256 devices in a mesh: wide: 32 (over x_hi, z, core), narrow: 8 (over y, x_lo).
Axes of the slice: x: 4 (x_hi: 2, x_lo: 2; x = x_hi * 2 + x_lo), y: 4, z: 8, core: 2. Of those that a mesh axis runs over, the one named last changes fastest.
Arguments:
- leaf_multipoles: float32 [8, 25, 64, 4096], P('narrow', None, 'wide'), may hold values from -6 to 6
- leaf_order: int32 [8, 64, 4096], P('narrow', 'wide'), may hold values from 2 to 4
- subtree_octant: int32 [8, 64, 4096], P('narrow', 'wide'), may hold values from 0 to 7, as said below
- m2m_operators: float32 [8, 25, 25], replicated, may hold values from -0.4375 to 0.4375
- coupling: float32 [25, 25], replicated, may hold values from -1.25 to 1.25
- kernel_spectrum: float32 [2, 9, 64, 64, 64], P(None, None, None, 'wide', 'narrow'), may hold values from -6 to 6
- l2l_operators: float32 [8, 25, 25], replicated, may hold values from -1.25 to 1.25
Outputs:
- leaf_locals: float32 [8, 25, 64, 4096], P('narrow', None, 'wide')
The draws below stay inside these ranges and needn't reach their ends.
Inputs may be any that keep to these rules, and one draw needn't show every extreme that they name: `subtree_octant`: for every coarse box the 8 slots hold its octants 0 to 7, each once.
All inputs are finite; a program needn't handle non-finite values.
Results may differ from the reference program's by a relative error of at most 0.0001.
Values sent between devices are 32-bit elements; how exact they have to be, the bound alone decides.
No kernel may reach another device: no remote copies, remote signals or barrier semaphores. Data moves between devices by JAX's collectives and lax.ppermute only.
A program may use at most 64 MiB of HBM per device.

```python
import jax
import jax.numpy as jnp
from jax import lax

ORDER = 4
GRID = 64
NCOEF = 25
KERNELS = 9


def draw_subtree_octant(key, part):
    key = jax.random.fold_in(key, 7)
    base = jnp.broadcast_to(jnp.arange(8, dtype=jnp.int32)[:, None], (8, GRID * GRID * GRID))
    mixed = jax.random.permutation(key, base, axis=0, independent=True)
    return mixed.reshape(8, GRID, GRID * GRID).astype(jnp.int32)


def place_ends(entries, own_key, low, largest):
    longest = entries.shape.index(max(entries.shape))
    spots = []
    for shift in (0, 1):
        where = [jax.random.randint(jax.random.fold_in(own_key, axis), (), 0, length) for axis, length in enumerate(entries.shape)]
        where[longest] = (where[longest] + shift) % entries.shape[longest]
        spots.append(tuple(where))
    return entries.at[spots[0]].set(low).at[spots[1]].set(largest)


def block_scale(key, extent, split, low, high):
    gain = 1.0
    for position, blocks in split:
        draws = jax.random.uniform(jax.random.fold_in(jax.random.fold_in(key, 6), position), (blocks,), jnp.float32, low / len(split), high / len(split))
        gain = gain * jnp.repeat(jnp.exp(draws), extent[position] // blocks).reshape((-1,) + (1,) * (len(extent) - 1 - position))
    return gain


def scatter_about(own_key, dims, deviation, bound, split=(), kind=jnp.bfloat16):
    values = deviation * jax.random.normal(own_key, dims, jnp.float32)
    if split:
        values = values * block_scale(own_key, dims, split, -0.22, 0.18)
    return jnp.clip(values, -bound, bound).astype(kind)


def setup_inputs(seed: int = 0) -> dict:
    keys = jax.random.split(jax.random.key(seed), 8)
    return {
        "leaf_multipoles": scatter_about(keys[0], (8, NCOEF, GRID, GRID * GRID), 1.0, 6.0, ((0, 8), (2, 32)), jnp.float32),
        "leaf_order": place_ends(jax.random.randint(keys[1], (8, GRID, GRID * GRID), ORDER // 2, ORDER + 1), jax.random.fold_in(keys[1], 1), ORDER // 2, ORDER).astype(jnp.int32),
        "subtree_octant": draw_subtree_octant(jax.random.fold_in(keys[7], 71), 0),
        "m2m_operators": scatter_about(keys[3], (8, NCOEF, NCOEF), (8 * NCOEF) ** -0.5, 0.4375, (), jnp.float32),
        "coupling": scatter_about(keys[4], (NCOEF, NCOEF), NCOEF ** -0.5, 1.25, (), jnp.float32),
        "kernel_spectrum": scatter_about(keys[5], (2, KERNELS, GRID, GRID, GRID), 1.0, 6.0, ((3, 32), (4, 8)), jnp.float32),
        "l2l_operators": scatter_about(keys[6], (8, NCOEF, NCOEF), NCOEF ** -0.5, 1.25, (), jnp.float32),
    }


exact_mode = lax.Precision.HIGHEST


def degree_list():
    return [degree for degree in range(ORDER + 1) for repeat in range(2 * degree + 1)]


def reference(leaf_multipoles, leaf_order, subtree_octant, m2m_operators, coupling, kernel_spectrum, l2l_operators):
    degree_of = jnp.array(degree_list(), jnp.int32)
    leaves = leaf_multipoles.reshape(8, NCOEF, GRID, GRID, GRID)
    orders = leaf_order.reshape(8, GRID, GRID, GRID)
    octants = subtree_octant.reshape(8, GRID, GRID, GRID)
    keep_mask = degree_of[None, :, None, None, None] <= orders[:, None]
    multipoles = jnp.zeros((NCOEF, GRID, GRID, GRID), jnp.float32)
    for octant in range(8):
        select = jnp.logical_and(keep_mask, (octants == octant)[:, None]).astype(jnp.float32)
        chosen = jnp.sum(leaves * select, axis=0)
        multipoles = multipoles + jnp.einsum("ac,cxyz->axyz", m2m_operators[octant], chosen, precision=exact_mode)
    spectrum = jnp.fft.fftn(multipoles, axes=(1, 2, 3))
    spec_real = jnp.real(spectrum)
    spec_imag = jnp.imag(spectrum)
    field_real = jnp.zeros_like(multipoles)
    field_imag = jnp.zeros_like(multipoles)
    for source in range(ORDER + 1):
        start_coef = source * source
        end_coef = start_coef + 2 * source + 1
        coupling_block = coupling[:, start_coef:end_coef]
        term_real = jnp.einsum("ac,cxyz->axyz", coupling_block, spec_real[start_coef:end_coef], precision=exact_mode)
        term_imag = jnp.einsum("ac,cxyz->axyz", coupling_block, spec_imag[start_coef:end_coef], precision=exact_mode)
        kernel_real = kernel_spectrum[0][degree_of + source]
        kernel_imag = kernel_spectrum[1][degree_of + source]
        field_real = field_real + kernel_real * term_real - kernel_imag * term_imag
        field_imag = field_imag + kernel_real * term_imag + kernel_imag * term_real
    local_field = jnp.real(jnp.fft.ifftn(lax.complex(field_real, field_imag), axes=(1, 2, 3)))
    products = jnp.stack([jnp.einsum("ac,cxyz->axyz", l2l_operators[octant], local_field, precision=exact_mode) for octant in range(8)], axis=0)
    children = jnp.take_along_axis(products, octants[:, None].astype(jnp.int32), axis=0)
    return children.reshape(8, NCOEF, GRID, GRID * GRID)
```

```python
import numpy as np
import ml_dtypes

import jax
import jax.numpy as jnp
from jax import lax
from jax.experimental import pallas as pl
from jax.experimental.pallas import tpu as pltpu
from jax.sharding import PartitionSpec as P

ORDER = 4
GRID = 64
NC = 25
SLOTS = 5
BF = jnp.bfloat16
F32 = jnp.float32
VMEM_LIMIT = 48 * 1024 * 1024

DEGREE = np.array([n for n in range(ORDER + 1) for _ in range(2 * n + 1)])


def halves(table):
    high = table.astype(ml_dtypes.bfloat16)
    low = (table - high.astype(np.float64)).astype(ml_dtypes.bfloat16)
    return high, low


def stack_left(table):
    high, low = halves(table)
    return np.concatenate([high, low, high], axis=1)


def stack_right(table):
    high, low = halves(table)
    return np.concatenate([high, low, high], axis=0)


def wave(a, b):
    angle = 2.0 * np.pi * ((a * b) % GRID) / GRID
    return np.cos(angle), np.sin(angle)


def complex_table(cosine, sine, sign):
    return np.stack([np.stack([cosine, -sign * sine]), np.stack([sign * sine, cosine])])


def z_tables():
    z = np.arange(GRID)
    forward, inverse = [], []
    for n in range(8):
        rows = []
        for t in range(SLOTS):
            for m in range(8):
                rows.append(8 * (n ^ m) + t)
        cosine, sine = wave(np.array(rows)[:, None], z[None, :])
        table = np.concatenate([cosine, -sine], axis=0)
        high, low = halves(table)
        forward.append(np.concatenate([high, low], axis=0))
        inverse.append(stack_left(table.T / GRID))
    return np.stack(forward), np.stack(inverse)


def y_tables():
    ky = np.arange(GRID)
    cosine, sine = wave(ky[:, None], ky[None, :])

    def place(table):
        table = table.reshape(2, 2, 32, 2, 32, 2)
        table = table.transpose(2, 3, 0, 1, 5, 4)
        full = np.zeros((32, 2, 2, 2, 2, 2, 32, 2))
        for xl in range(2):
            full[:, xl, :, :, :, :, :, xl] = table
        return full.reshape(256, 256)

    forward = place(complex_table(cosine, sine, -1))
    back = complex_table(cosine, sine, 1) / GRID
    inverse = place(back.transpose(1, 0, 2, 3))
    return stack_left(forward), stack_right(inverse)


def x_tables():
    kx = np.arange(GRID)
    cosine, sine = wave(kx[:, None], kx[None, :])

    def place(table):
        table = table.reshape(2, 2, GRID, 32, 2).transpose(0, 2, 3, 4, 1)
        full = np.zeros((2, 2, GRID, 32, 2, 2, 2))
        for k2 in range(2):
            full[k2, :, :, :, :, k2, :] = table
        return full.reshape(256, 256)

    forward = place(complex_table(cosine, sine, -1))
    back = complex_table(cosine, sine, 1) / GRID
    inverse = place(back.transpose(1, 0, 2, 3)).T
    return stack_left(forward), stack_left(inverse)


def expand_tables():
    own = np.zeros((72, 640), np.float32)
    mirror = np.zeros((72, 640), np.float32)
    rows = np.zeros((128, NC), np.float32)
    lanes = np.zeros((NC, 640), np.float32)
    mask = np.zeros((128, 640), np.float32)
    for t in range(SLOTS):
        for c in range(NC):
            rows[t * NC + c, c] = 1
            for s in range(ORDER + 1):
                lane = s * 128 + t * NC + c
                lanes[c, lane] = 1
                d = DEGREE[c] + s
                own[d * 8 + t, lane] = 1
                if 1 <= t <= 3:
                    mirror[d * 8 + 8 - t, lane] = 1
                for j in range(NC):
                    if DEGREE[j] == s:
                        mask[t * NC + j, lane] = 1
    flip = np.zeros((GRID, GRID), np.float32)
    for k in range(GRID):
        flip[(-k) % GRID, k] = 1
    return np.concatenate([own, mirror], axis=0), rows, lanes, mask, flip


def split(value):
    high = value.astype(BF)
    low = (value - high.astype(F32)).astype(BF)
    return high, low


def stacked(value, axis):
    high, low = split(value)
    return jnp.concatenate([high, high, low], axis=axis)


def dot(a, b, dims=((1,), (0,)), precision=None):
    return lax.dot_general(a, b, (dims, ((), ())), precision=precision, preferred_element_type=F32)


def degree_column():
    row = lax.broadcasted_iota(jnp.int32, (32, 1), 0)
    one = lambda bound: (row >= bound).astype(jnp.int32)
    return one(1) + one(4) + one(9) + one(16) + 90 * one(25)


def load_operators(op_ref, w_ref):
    w_ref[...] = jnp.zeros_like(w_ref)
    w_ref[0:200, 0:NC] = op_ref[...]
    rows = [w_ref[pl.ds(octant, 32, stride=8), :][:, 0:32] for octant in range(8)]
    high, low = split(jnp.concatenate(rows, axis=0))
    return jnp.concatenate([high, low, high], axis=1)


def lane_rows(ref, first, count):
    return jnp.concatenate([ref[pl.ds(first + i, 1), :] for i in range(count)], axis=1)


def translate(w_cat, value, octant):
    product = dot(w_cat, stacked(value, 0))
    total = product[0:32]
    for o in range(1, 8):
        total = jnp.where(octant == o, product[32 * o : 32 * o + 32], total)
    return total


GROUP = 4


def head_kernel(leaf_ref, order_ref, octant_ref, op_ref, table_ref, out_ref, xs, ws, ms, sem):
    copy = pltpu.make_async_copy(leaf_ref, xs.at[pl.ds(0, NC * 64)], sem)
    copy.start()
    w_cat = load_operators(op_ref, ws)
    degree = degree_column()
    me = lax.axis_index("narrow")
    table = table_ref[me]
    for m in range(16):
        out_ref[m * 128 + 120 : m * 128 + 128, :] = jnp.zeros((8, 128), F32)
    copy.wait()

    def group(g, carry):
        b = g * GROUP
        x = jnp.concatenate([xs[pl.ds(b + i, 32, stride=64), :] for i in range(GROUP)], axis=1)
        kept = jnp.where(degree <= lane_rows(order_ref, b, GROUP), x, 0.0)
        total = translate(w_cat, kept, lane_rows(octant_ref, b, GROUP))
        for i in range(GROUP):
            ms[pl.ds(b + i, NC, stride=64), :] = total[0:NC, 128 * i : 128 * i + 128]
        return carry

    lax.fori_loop(0, 64 // GROUP, group, 0)

    def coefficient(c, carry):
        plane = ms[pl.ds(pl.multiple_of(c * 64, 64), 64), :]
        plane = jnp.concatenate([plane[:, 0:64], plane[:, 64:128]], axis=0)
        high, low = split(plane)
        both = dot(table, high, ((1,), (1,)))
        result = both[0:80] + both[80:160] + dot(table[0:80], low, ((1,), (1,)))
        for p in range(2):
            for t in range(SLOTS):
                row = 40 * p + 8 * t
                out_ref[pl.ds(p * 128 + t * NC + c, 8, stride=256), :] = result[row : row + 8]
        return carry

    lax.fori_loop(0, NC, coefficient, 0)


def y_forward_kernel(*refs):
    *parts, table_ref, out_ref = refs
    total = parts[0][...]
    for part in parts[1:]:
        total = total + part[...]
    total = jnp.concatenate([total[0:128], total[128:256]], axis=1)
    out_ref[...] = dot(table_ref[...], stacked(total, 1), ((1,), (1,)))


def prepare_kernel(k_ref, r0_ref, r1_ref, coupling_ref, expand_ref, rows_ref, lanes_ref, mask_ref, flip_ref, k_out, c_out):
    exact = lax.Precision.HIGHEST
    for part in range(2):
        for k2 in range(2):
            own = k_ref[part, :, k2].reshape(72, GRID)
            mirror = (r0_ref, r1_ref)[k2][part].reshape(72, GRID)
            mirror = dot(mirror, flip_ref[...], precision=exact)
            if part == 1:
                mirror = -mirror
            both = jnp.concatenate([own, mirror], axis=0).T
            k_out[part, k2 * 64 : k2 * 64 + 64, :] = dot(both, expand_ref[...], precision=exact)
    spread = dot(coupling_ref[...], lanes_ref[...], ((0,), (0,)), precision=exact)
    spread = dot(rows_ref[...], spread, precision=exact) * mask_ref[...]
    high, low = split(spread)
    c_out[...] = jnp.concatenate([high, low, high], axis=0)


def middle_kernel(a_ref, forward_ref, c_ref, k_ref, inverse_ref, out_ref):
    freq = dot(forward_ref[...], stacked(a_ref[...], 0))
    terms = dot(stacked(freq, 1), c_ref[...])
    pieces = []
    for k2 in range(2):
        real = jnp.zeros((64, 128), F32)
        imag = jnp.zeros((64, 128), F32)
        for s in range(ORDER + 1):
            lanes = slice(128 * s, 128 * s + 128)
            tr = terms[k2 * 128 : k2 * 128 + 64, lanes]
            ti = terms[k2 * 128 + 64 : k2 * 128 + 128, lanes]
            kr = k_ref[0, k2 * 64 : k2 * 64 + 64, lanes]
            ki = k_ref[1, k2 * 64 : k2 * 64 + 64, lanes]
            real = real + kr * tr - ki * ti
            imag = imag + kr * ti + ki * tr
        pieces += [real, imag]
    field = jnp.concatenate(pieces, axis=0)
    out_ref[...] = dot(inverse_ref[...], stacked(field, 0))


def y_inverse_kernel(a_ref, table_ref, out_ref):
    result = dot(stacked(a_ref[...].T, 1), table_ref[...])
    out_ref[0:128, :] = result[:, 0:128]
    out_ref[128:256, :] = result[:, 128:256]


def tail_kernel(*refs):
    parts = refs[0:8]
    octant_ref, op_ref, table_ref, out_ref, fs, ws, ls = refs[8:]
    for m in range(8):
        fs[m * 256 : m * 256 + 256, :] = parts[m][...]
    w_cat = load_operators(op_ref, ws)
    ls[pl.ds(NC * 64, 7 * 64), :] = jnp.zeros((7 * 64, 128), F32)
    me = lax.axis_index("narrow")
    table = table_ref[me]

    def coefficient(c, carry):
        rows = []
        for p in range(2):
            for t in range(SLOTS):
                rows.append(fs[pl.ds(p * 128 + t * NC + c, 8, stride=256), :])
        freq = jnp.concatenate(rows, axis=0)
        plane = dot(table, stacked(freq, 0)).T
        ls[pl.ds(pl.multiple_of(c * 64, 64), 64), :] = jnp.concatenate([plane[0:64], plane[64:128]], axis=1)
        return carry

    lax.fori_loop(0, NC, coefficient, 0)

    def group(g, carry):
        b = g * GROUP
        x = jnp.concatenate([ls[pl.ds(b + i, 32, stride=64), :] for i in range(GROUP)], axis=1)
        total = translate(w_cat, x, lane_rows(octant_ref, b, GROUP))
        for i in range(GROUP):
            out_ref[pl.ds(b + i, NC, stride=64), :] = total[0:NC, 128 * i : 128 * i + 128]
        return carry

    lax.fori_loop(0, 64 // GROUP, group, 0)


def call(kernel, out_shape, scratch=(), in_specs=None):
    args = {}
    if in_specs is not None:
        args["in_specs"] = in_specs
    return pl.pallas_call(
        kernel,
        out_shape=out_shape,
        scratch_shapes=list(scratch),
        compiler_params=pltpu.CompilerParams(vmem_limit_bytes=VMEM_LIMIT),
        **args,
    )


def shape(*dims, dtype=F32):
    return jax.ShapeDtypeStruct(dims, dtype)


Z_FORWARD, Z_INVERSE = z_tables()
Y_FORWARD, Y_INVERSE = y_tables()
X_FORWARD, X_INVERSE = x_tables()
EXPAND, ROWS, LANES, MASK, FLIP = expand_tables()


def block_rows(array):
    lead = array.shape[:-2]
    array = array.reshape(lead + (2, 32, 128))
    array = jnp.swapaxes(array, -3, -2)
    return array.reshape(-1, 128)


def swap(array, m):
    return lax.ppermute(array, "narrow", [(i, i ^ m) for i in range(8)])


def shards(leaf_multipoles, leaf_order, subtree_octant, m2m_operators, coupling, kernel_spectrum, l2l_operators):
    leaves = block_rows(leaf_multipoles[0])
    orders = block_rows(leaf_order[0])
    octants = block_rows(subtree_octant[0])
    m2m = jnp.swapaxes(m2m_operators, 0, 1).reshape(NC * 8, NC)
    l2l = jnp.swapaxes(l2l_operators, 0, 1).reshape(NC * 8, NC)
    kernel = kernel_spectrum.transpose(0, 1, 3, 4, 2)

    to_even = [(w * 8 + n, ((32 - w) % 32) * 8 + 7 - n) for w in range(32) for n in range(8)]
    to_odd = [(w * 8 + n, (31 - w) * 8 + 7 - n) for w in range(32) for n in range(8)]
    mirror0 = lax.ppermute(kernel[:, :, 0], ("wide", "narrow"), to_even)
    mirror1 = lax.ppermute(kernel[:, :, 1], ("wide", "narrow"), to_odd)

    vmem = pl.BlockSpec(memory_space=pltpu.VMEM)
    chunks = call(
        head_kernel,
        shape(2048, 128),
        [pltpu.VMEM((2048, 128), F32), pltpu.VMEM((256, 128), F32), pltpu.VMEM((NC * 64, 128), F32), pltpu.SemaphoreType.DMA],
        [pl.BlockSpec(memory_space=pl.ANY)] + [vmem] * 4,
    )(leaves, orders, octants, m2m, jnp.asarray(Z_FORWARD))
    chunks = chunks.reshape(8, 256, 128)
    received = [chunks[0]] + [swap(chunks[m], m) for m in range(1, 8)]

    kernels, couplings = call(prepare_kernel, (shape(2, 128, 640), shape(384, 640, dtype=BF)))(
        kernel, mirror0, mirror1, coupling,
        jnp.asarray(EXPAND), jnp.asarray(ROWS), jnp.asarray(LANES), jnp.asarray(MASK), jnp.asarray(FLIP),
    )

    along = call(y_forward_kernel, shape(256, 128))(*received, jnp.asarray(Y_FORWARD))
    along = lax.all_to_all(along.reshape(32, 8, 128), "wide", split_axis=0, concat_axis=0, tiled=True)
    along = call(middle_kernel, shape(256, 128))(
        along.reshape(256, 128), jnp.asarray(X_FORWARD), couplings, kernels, jnp.asarray(X_INVERSE)
    )
    along = lax.all_to_all(along.reshape(32, 8, 128), "wide", split_axis=0, concat_axis=0, tiled=True)
    plane = call(y_inverse_kernel, shape(256, 128))(along.reshape(256, 128), jnp.asarray(Y_INVERSE))

    planes = [plane] + [swap(plane, m) for m in range(1, 8)]
    children = call(
        tail_kernel,
        shape(NC * 64, 128),
        [pltpu.VMEM((2048, 128), F32), pltpu.VMEM((256, 128), F32), pltpu.VMEM((2048, 128), F32)],
    )(*planes, octants, l2l, jnp.asarray(Z_INVERSE))
    children = children.reshape(NC, 32, 2, 128).swapaxes(1, 2)
    return children.reshape(1, NC, 2, 4096)


def solution(mesh):
    return jax.shard_map(
        shards,
        mesh=mesh,
        in_specs=(
            P("narrow", None, "wide", None),
            P("narrow", "wide", None),
            P("narrow", "wide", None),
            P(),
            P(),
            P(None, None, None, "wide", "narrow"),
            P(),
        ),
        out_specs=P("narrow", None, "wide", None),
        check_vma=False,
    )
```

```python
import numpy as np
import ml_dtypes

import jax
import jax.numpy as jnp
from jax import lax
from jax.experimental import pallas as pl
from jax.experimental.pallas import tpu as pltpu
from jax.sharding import PartitionSpec as P

ORDER = 4
GRID = 64
NC = 25
SLOTS = 5
BF = jnp.bfloat16
F32 = jnp.float32
VMEM_LIMIT = 48 * 1024 * 1024

STEPS = ((0, 0), (2, 0), (1, 0), (-1, 0), (0, 1), (2, 1), (1, 1), (-1, 1))

DEGREE = np.array([n for n in range(ORDER + 1) for _ in range(2 * n + 1)])


def halves(table):
    high = table.astype(ml_dtypes.bfloat16)
    low = (table - high.astype(np.float64)).astype(ml_dtypes.bfloat16)
    return high, low


def stack_left(table):
    high, low = halves(table)
    return np.concatenate([high, low, high], axis=1)


def stack_right(table):
    high, low = halves(table)
    return np.concatenate([high, low, high], axis=0)


def wave(a, b):
    angle = 2.0 * np.pi * ((a * b) % GRID) / GRID
    return np.cos(angle), np.sin(angle)


def complex_table(cosine, sine, sign):
    return np.stack([np.stack([cosine, -sign * sine]), np.stack([sign * sine, cosine])])


def stepped(n, step, sign):
    return (n // 2 + sign * step[0]) % 4 * 2 + (n + step[1]) % 2


def z_tables():
    z = np.arange(GRID)
    forward, inverse = [], []
    for n in range(8):
        tables = []
        for sign in (1, -1):
            rows = [8 * stepped(n, step, sign) + t for t in range(SLOTS) for step in STEPS]
            cosine, sine = wave(np.array(rows)[:, None], z[None, :])
            tables.append(np.concatenate([cosine, -sine], axis=0))
        forward.append(stack_left(tables[0]))
        inverse.append(stack_left(tables[1].T / GRID))
    return np.stack(forward), np.stack(inverse)


def y_tables():
    ky = np.arange(GRID)
    cosine, sine = wave(ky[:, None], ky[None, :])

    def place(table):
        table = table.reshape(2, 2, 32, 2, 32, 2)
        table = table.transpose(2, 3, 0, 1, 5, 4)
        full = np.zeros((32, 2, 2, 2, 2, 2, 32, 2))
        for xl in range(2):
            full[:, xl, :, :, :, :, :, xl] = table
        return full.reshape(256, 256)

    forward = place(complex_table(cosine, sine, -1))
    back = complex_table(cosine, sine, 1) / GRID
    inverse = place(back.transpose(1, 0, 2, 3))
    return stack_left(forward), stack_right(inverse)


def x_tables():
    kx = np.arange(GRID)
    cosine, sine = wave(kx[:, None], kx[None, :])

    def place(table):
        table = table.reshape(2, 2, GRID, 32, 2).transpose(0, 2, 3, 4, 1)
        full = np.zeros((2, 2, GRID, 32, 2, 2, 2))
        for k2 in range(2):
            full[k2, :, :, :, :, k2, :] = table
        return full.reshape(256, 256)

    forward = place(complex_table(cosine, sine, -1))
    back = complex_table(cosine, sine, 1) / GRID
    inverse = place(back.transpose(1, 0, 2, 3)).T
    return stack_left(forward), stack_left(inverse)


def expand_tables():
    own = np.zeros((72, 640), np.float32)
    mirror = np.zeros((72, 640), np.float32)
    rows = np.zeros((128, NC), np.float32)
    lanes = np.zeros((NC, 640), np.float32)
    mask = np.zeros((128, 640), np.float32)
    for t in range(SLOTS):
        for c in range(NC):
            rows[t * NC + c, c] = 1
            for s in range(ORDER + 1):
                lane = s * 128 + t * NC + c
                lanes[c, lane] = 1
                d = DEGREE[c] + s
                own[d * 8 + t, lane] = 1
                if 1 <= t <= 3:
                    mirror[d * 8 + 8 - t, lane] = 1
                for j in range(NC):
                    if DEGREE[j] == s:
                        mask[t * NC + j, lane] = 1
    flip = np.zeros((GRID, GRID), np.float32)
    for k in range(GRID):
        flip[(-k) % GRID, k] = 1
    return np.concatenate([own, mirror], axis=0), rows, lanes, mask, flip


def split(value):
    high = value.astype(BF)
    low = (value - high.astype(F32)).astype(BF)
    return high, low


def stacked(value, axis):
    high, low = split(value)
    return jnp.concatenate([high, high, low], axis=axis)


def dot(a, b, dims=((1,), (0,)), precision=None):
    return lax.dot_general(a, b, (dims, ((), ())), precision=precision, preferred_element_type=F32)


def degree_column():
    row = lax.broadcasted_iota(jnp.int32, (32, 1), 0)
    one = lambda bound: (row >= bound).astype(jnp.int32)
    return one(1) + one(4) + one(9) + one(16) + 90 * one(25)


def load_operators(op_ref, w_ref):
    w_ref[...] = jnp.zeros_like(w_ref)
    w_ref[0:200, 0:NC] = op_ref[...]
    rows = [w_ref[pl.ds(octant, 32, stride=8), :][:, 0:32] for octant in range(8)]
    high, low = split(jnp.concatenate(rows, axis=0))
    return jnp.concatenate([high, low, high], axis=1)


def lane_rows(ref, first, count):
    return jnp.concatenate([ref[pl.ds(first + i, 1), :] for i in range(count)], axis=1)


def translate(w_cat, value, octant):
    product = dot(w_cat, stacked(value, 0))
    total = product[0:32]
    for o in range(1, 8):
        total = jnp.where(octant == o, product[32 * o : 32 * o + 32], total)
    return total


GROUP = 8
BATCH = 5


def head_kernel(leaf_hbm, order_hbm, octant_hbm, op_hbm, ms, xs, order_ref, octant_ref, op_ref, ws, sems):
    copies = [
        pltpu.make_async_copy(op_hbm, op_ref, sems.at[0]),
        pltpu.make_async_copy(leaf_hbm, xs.at[pl.ds(0, NC * 64)], sems.at[1]),
        pltpu.make_async_copy(order_hbm, order_ref, sems.at[2]),
        pltpu.make_async_copy(octant_hbm, octant_ref, sems.at[3]),
    ]
    for copy in copies:
        copy.start()
    copies[0].wait()
    w_cat = load_operators(op_ref, ws)
    degree = degree_column()
    for copy in copies[1:]:
        copy.wait()

    def group(g, carry):
        b = g * GROUP
        x = jnp.concatenate([xs[pl.ds(b + i, 32, stride=64), :] for i in range(GROUP)], axis=1)
        kept = jnp.where(degree <= lane_rows(order_ref, b, GROUP), x, 0.0)
        total = translate(w_cat, kept, lane_rows(octant_ref, b, GROUP))
        for i in range(GROUP):
            ms[pl.ds(b + i, NC, stride=64), :] = total[0:NC, 128 * i : 128 * i + 128]
        return carry

    lax.fori_loop(0, 64 // GROUP, group, 0)


def z_forward_kernel(ms, table_ref, _0, _1, out_ref):
    me = lax.axis_index("narrow")
    table = table_ref[me]
    for m in range(16):
        out_ref[m * 128 + 120 : m * 128 + 128, :] = jnp.zeros((8, 128), F32)

    def coefficients(g, carry):
        first = g * BATCH
        rows = pl.ds(pl.multiple_of(first * 64, 64), 64 * BATCH)
        pieces = []
        for part in split(ms[rows, :]):
            halves_ = [part[64 * i : 64 * i + 64, 64 * y2 : 64 * y2 + 64] for i in range(BATCH) for y2 in range(2)]
            pieces.append(jnp.concatenate(halves_, axis=0))
        high, low = pieces
        result = dot(table, jnp.concatenate([high, high, low], axis=1), ((1,), (1,)))
        for i in range(BATCH):
            for p in range(2):
                for t in range(SLOTS):
                    row = 40 * p + 8 * t
                    value = result[row : row + 8, 128 * i : 128 * i + 128]
                    out_ref[pl.ds(p * 128 + t * NC + first + i, 8, stride=256), :] = value
        return carry

    lax.fori_loop(0, NC // BATCH, coefficients, 0)


def y_forward_kernel(*refs):
    *parts, table_ref, _, out_ref = refs
    total = parts[0][...]
    for part in parts[1:]:
        total = total + part[...]
    total = jnp.concatenate([total[0:128], total[128:256]], axis=1)
    out_ref[...] = dot(table_ref[...], stacked(total, 1), ((1,), (1,)))


def prepare_kernel(k_ref, r0_ref, r1_ref, coupling_ref, expand_ref, rows_ref, lanes_ref, mask_ref, flip_ref, k_out, c_out):
    exact = lax.Precision.HIGHEST
    for part in range(2):
        for k2 in range(2):
            own = k_ref[part, :, k2].reshape(72, GRID)
            mirror = (r0_ref, r1_ref)[k2][part].reshape(72, GRID)
            mirror = dot(mirror, flip_ref[...], precision=exact)
            if part == 1:
                mirror = -mirror
            both = jnp.concatenate([own, mirror], axis=0).T
            k_out[part, k2 * 64 : k2 * 64 + 64, :] = dot(both, expand_ref[...], precision=exact)
    spread = dot(coupling_ref[...], lanes_ref[...], ((0,), (0,)), precision=exact)
    spread = dot(rows_ref[...], spread, precision=exact) * mask_ref[...]
    high, low = split(spread)
    c_out[...] = jnp.concatenate([high, low, high], axis=0)


def middle_kernel(a_ref, forward_ref, c_ref, k_ref, inverse_ref, out_ref):
    freq = dot(forward_ref[...], stacked(a_ref[...], 0))
    terms = dot(stacked(freq, 1), c_ref[...])
    pieces = []
    for k2 in range(2):
        real = jnp.zeros((64, 128), F32)
        imag = jnp.zeros((64, 128), F32)
        for s in range(ORDER + 1):
            lanes = slice(128 * s, 128 * s + 128)
            tr = terms[k2 * 128 : k2 * 128 + 64, lanes]
            ti = terms[k2 * 128 + 64 : k2 * 128 + 128, lanes]
            kr = k_ref[0, k2 * 64 : k2 * 64 + 64, lanes]
            ki = k_ref[1, k2 * 64 : k2 * 64 + 64, lanes]
            real = real + kr * tr - ki * ti
            imag = imag + kr * ti + ki * tr
        pieces += [real, imag]
    field = jnp.concatenate(pieces, axis=0)
    out_ref[...] = dot(inverse_ref[...], stacked(field, 0))


def y_inverse_kernel(a_ref, table_ref, out_ref):
    result = dot(stacked(a_ref[...].T, 1), table_ref[...])
    out_ref[0:128, :] = result[:, 0:128]
    out_ref[128:256, :] = result[:, 128:256]


def z_inverse_kernel(*refs):
    parts = refs[0:8]
    table_ref, ls, fs = refs[8:]
    for m in range(8):
        fs[m * 256 : m * 256 + 256, :] = parts[m][...]
    ls[pl.ds(NC * 64, 7 * 64), :] = jnp.zeros((7 * 64, 128), F32)
    me = lax.axis_index("narrow")
    table = table_ref[me]

    def coefficients(g, carry):
        first = g * BATCH
        freqs = []
        for i in range(BATCH):
            rows = []
            for p in range(2):
                for t in range(SLOTS):
                    rows.append(fs[pl.ds(p * 128 + t * NC + first + i, 8, stride=256), :])
            freqs.append(jnp.concatenate(rows, axis=0))
        result = dot(table, stacked(jnp.concatenate(freqs, axis=1), 0))
        for i in range(BATCH):
            plane = result[:, 128 * i : 128 * i + 128].T
            rows = pl.ds(pl.multiple_of((first + i) * 64, 64), 64)
            ls[rows, :] = jnp.concatenate([plane[0:64], plane[64:128]], axis=1)
        return carry

    lax.fori_loop(0, NC // BATCH, coefficients, 0)


def tail_kernel(ls, octant_ref, op_ref, out_ref, ws):
    w_cat = load_operators(op_ref, ws)

    def group(g, carry):
        b = g * GROUP
        x = jnp.concatenate([ls[pl.ds(b + i, 32, stride=64), :] for i in range(GROUP)], axis=1)
        total = translate(w_cat, x, lane_rows(octant_ref, b, GROUP))
        for i in range(GROUP):
            out_ref[pl.ds(b + i, NC, stride=64), :] = total[0:NC, 128 * i : 128 * i + 128]
        return carry

    lax.fori_loop(0, 64 // GROUP, group, 0)


def call(kernel, out_shape, scratch=(), in_specs=None):
    args = {}
    if in_specs is not None:
        args["in_specs"] = in_specs
    return pl.pallas_call(
        kernel,
        out_shape=out_shape,
        scratch_shapes=list(scratch),
        compiler_params=pltpu.CompilerParams(vmem_limit_bytes=VMEM_LIMIT),
        **args,
    )


def shape(*dims, dtype=F32):
    return jax.ShapeDtypeStruct(dims, dtype)


Z_FORWARD, Z_INVERSE = z_tables()
Y_FORWARD, Y_INVERSE = y_tables()
X_FORWARD, X_INVERSE = x_tables()
EXPAND, ROWS, LANES, MASK, FLIP = expand_tables()


def block_rows(array):
    lead = array.shape[:-2]
    array = array.reshape(lead + (2, 32, 128))
    array = jnp.swapaxes(array, -3, -2)
    return array.reshape(-1, 128)


def shift(array, step):
    return lax.ppermute(array, "narrow", [(n, stepped(n, step, 1)) for n in range(8)])


def shards(leaf_multipoles, leaf_order, subtree_octant, m2m_operators, coupling, kernel_spectrum, l2l_operators):
    leaves = block_rows(leaf_multipoles[0])
    orders = block_rows(leaf_order[0])
    octants = block_rows(subtree_octant[0])
    m2m = jnp.swapaxes(m2m_operators, 0, 1).reshape(NC * 8, NC)
    l2l = jnp.swapaxes(l2l_operators, 0, 1).reshape(NC * 8, NC)
    kernel = kernel_spectrum.transpose(0, 1, 3, 4, 2)

    to_even = [(w * 8 + n, ((32 - w) % 32) * 8 + 7 - n) for w in range(32) for n in range(8)]
    to_odd = [(w * 8 + n, (31 - w) * 8 + 7 - n) for w in range(32) for n in range(8)]
    mirror0 = lax.ppermute(kernel[:, :, 0], ("wide", "narrow"), to_even)
    mirror1 = lax.ppermute(kernel[:, :, 1], ("wide", "narrow"), to_odd)

    chunks = call(
        head_kernel,
        shape(NC * 64, 128),
        [
            pltpu.VMEM((2048, 128), F32),
            pltpu.VMEM((64, 128), jnp.int32),
            pltpu.VMEM((64, 128), jnp.int32),
            pltpu.VMEM((NC * 8, NC), F32),
            pltpu.VMEM((256, 128), F32),
            pltpu.SemaphoreType.DMA((4,)),
        ],
        [pl.BlockSpec(memory_space=pltpu.HBM)] * 4,
    )(leaves, orders, octants, m2m)
    whole = pl.BlockSpec(memory_space=pltpu.VMEM)
    anywhere = pl.BlockSpec(memory_space=pl.ANY)
    chunks = call(z_forward_kernel, shape(2048, 128), (), [whole] * 2 + [anywhere] * 2)(
        chunks, jnp.asarray(Z_FORWARD), mirror0, mirror1
    )
    chunks = chunks.reshape(8, 256, 128)
    across = chunks[4] + sum(shift(chunks[4 + m], STEPS[m]) for m in (1, 2, 3))
    received = [chunks[0]] + [shift(chunks[m], STEPS[m]) for m in (1, 2, 3)] + [shift(across, STEPS[4])]

    kernels, couplings = call(prepare_kernel, (shape(2, 128, 640), shape(384, 640, dtype=BF)))(
        kernel, mirror0, mirror1, coupling,
        jnp.asarray(EXPAND), jnp.asarray(ROWS), jnp.asarray(LANES), jnp.asarray(MASK), jnp.asarray(FLIP),
    )

    along = call(y_forward_kernel, shape(256, 128), (), [whole] * 6 + [anywhere])(*received, jnp.asarray(Y_FORWARD), kernels)
    along = lax.all_to_all(along.reshape(32, 8, 128), "wide", split_axis=0, concat_axis=0, tiled=True)
    along = call(middle_kernel, shape(256, 128))(
        along.reshape(256, 128), jnp.asarray(X_FORWARD), couplings, kernels, jnp.asarray(X_INVERSE)
    )
    along = lax.all_to_all(along.reshape(32, 8, 128), "wide", split_axis=0, concat_axis=0, tiled=True)
    plane = call(y_inverse_kernel, shape(256, 128))(along.reshape(256, 128), jnp.asarray(Y_INVERSE))

    other = shift(plane, STEPS[4])
    planes = [plane] + [shift(plane, STEPS[m]) for m in (1, 2, 3)]
    planes += [other] + [shift(other, STEPS[m]) for m in (1, 2, 3)]
    local = call(z_inverse_kernel, shape(2048, 128), [pltpu.VMEM((2048, 128), F32)])(*planes, jnp.asarray(Z_INVERSE))
    children = call(tail_kernel, shape(NC * 64, 128), [pltpu.VMEM((256, 128), F32)])(local, octants, l2l)
    children = children.reshape(NC, 32, 2, 128).swapaxes(1, 2)
    return children.reshape(1, NC, 2, 4096)


def solution(mesh):
    return jax.shard_map(
        shards,
        mesh=mesh,
        in_specs=(
            P("narrow", None, "wide", None),
            P("narrow", "wide", None),
            P("narrow", "wide", None),
            P(),
            P(),
            P(None, None, None, "wide", "narrow"),
            P(),
        ),
        out_specs=P("narrow", None, "wide", None),
        check_vma=False,
    )
```

```python
import numpy as np
import ml_dtypes

import jax
import jax.numpy as jnp
from jax import lax
from jax.experimental import pallas as pl
from jax.experimental.pallas import tpu as pltpu
from jax.sharding import PartitionSpec as P

ORDER = 4
GRID = 64
NC = 25
SLOTS = 5
BF = jnp.bfloat16
F32 = jnp.float32
VMEM_LIMIT = 48 * 1024 * 1024

STEPS = ((0, 0), (2, 0), (1, 0), (-1, 0), (0, 1), (2, 1), (1, 1), (-1, 1))
_, FAR, ABOVE, BELOW, ACROSS = STEPS[:5]

DEGREE = np.array([n for n in range(ORDER + 1) for _ in range(2 * n + 1)])


def halves(table):
    high = table.astype(ml_dtypes.bfloat16)
    low = (table - high.astype(np.float64)).astype(ml_dtypes.bfloat16)
    return high, low


def stack_left(table):
    high, low = halves(table)
    return np.concatenate([high, low, high], axis=1)


def stack_right(table):
    high, low = halves(table)
    return np.concatenate([high, low, high], axis=0)


def wave(a, b):
    angle = 2.0 * np.pi * ((a * b) % GRID) / GRID
    return np.cos(angle), np.sin(angle)


def complex_table(cosine, sine, sign):
    return np.stack([np.stack([cosine, -sign * sine]), np.stack([sign * sine, cosine])])


def stepped(n, step, sign):
    return (n // 2 + sign * step[0]) % 4 * 2 + (n + step[1]) % 2


def z_tables():
    z = np.arange(GRID)
    forward, inverse = [], []
    for n in range(8):
        tables = []
        for sign in (1, -1):
            rows = [8 * stepped(n, step, sign) + t for t in range(SLOTS) for step in STEPS]
            cosine, sine = wave(np.array(rows)[:, None], z[None, :])
            tables.append(np.concatenate([cosine, -sine], axis=0))
        forward.append(stack_left(tables[0]))
        inverse.append(stack_left(tables[1].T / GRID))
    return np.stack(forward), np.stack(inverse)


def y_tables():
    ky = np.arange(GRID)
    cosine, sine = wave(ky[:, None], ky[None, :])

    def place(table):
        table = table.reshape(2, 2, 32, 2, 32, 2)
        table = table.transpose(2, 3, 0, 1, 5, 4)
        full = np.zeros((32, 2, 2, 2, 2, 2, 32, 2))
        for xl in range(2):
            full[:, xl, :, :, :, :, :, xl] = table
        return full.reshape(256, 256)

    forward = place(complex_table(cosine, sine, -1))
    back = complex_table(cosine, sine, 1) / GRID
    inverse = place(back.transpose(1, 0, 2, 3))
    return stack_left(forward), stack_right(inverse)


def x_tables():
    kx = np.arange(GRID)
    cosine, sine = wave(kx[:, None], kx[None, :])

    def place(table):
        table = table.reshape(2, 2, GRID, 32, 2).transpose(0, 2, 3, 4, 1)
        full = np.zeros((2, 2, GRID, 32, 2, 2, 2))
        for k2 in range(2):
            full[k2, :, :, :, :, k2, :] = table
        return full.reshape(256, 256)

    forward = place(complex_table(cosine, sine, -1))
    back = complex_table(cosine, sine, 1) / GRID
    inverse = place(back.transpose(1, 0, 2, 3)).T
    return stack_left(forward), stack_left(inverse)


def expand_tables():
    own = np.zeros((72, 640), np.float32)
    mirror = np.zeros((32, 640), np.float32)
    rows = np.zeros((128, NC), np.float32)
    lanes = np.zeros((NC, 640), np.float32)
    mask = np.zeros((128, 640), np.float32)
    for t in range(SLOTS):
        for c in range(NC):
            rows[t * NC + c, c] = 1
            for s in range(ORDER + 1):
                lane = s * 128 + t * NC + c
                lanes[c, lane] = 1
                d = DEGREE[c] + s
                own[d * 8 + t, lane] = 1
                if 1 <= t <= 3:
                    mirror[(3 - t) * 9 + d, lane] = 1
                for j in range(NC):
                    if DEGREE[j] == s:
                        mask[t * NC + j, lane] = 1
    flip = np.zeros((GRID, GRID), np.float32)
    for k in range(GRID):
        flip[(-k) % GRID, k] = 1
    return np.concatenate([own, mirror], axis=0), rows, lanes, mask, flip


def split(value):
    high = value.astype(BF)
    low = (value - high.astype(F32)).astype(BF)
    return high, low


def stacked(value, axis):
    high, low = split(value)
    return jnp.concatenate([high, high, low], axis=axis)


def dot(a, b, dims=((1,), (0,)), precision=None):
    return lax.dot_general(a, b, (dims, ((), ())), precision=precision, preferred_element_type=F32)


def degree_column():
    row = lax.broadcasted_iota(jnp.int32, (32, 1), 0)
    one = lambda bound: (row >= bound).astype(jnp.int32)
    return one(1) + one(4) + one(9) + one(16) + 90 * one(25)


def load_operators(op_ref, w_ref):
    w_ref[...] = jnp.zeros_like(w_ref)
    w_ref[0:200, 0:NC] = op_ref[...]
    rows = [w_ref[pl.ds(octant, 24, stride=8), :] for octant in range(8)] + [w_ref[192:200, :]]
    high, low = split(jnp.concatenate(rows, axis=0)[:, 0:32])
    return jnp.concatenate([high, low, high], axis=1)


def load_blocks(ref, first):
    blocks = []
    for i in range(GROUP):
        last = ref[pl.ds(24 * 64 + first + i, 1), :]
        blocks.append(jnp.concatenate([ref[pl.ds(first + i, 24, stride=64), :], jnp.broadcast_to(last, (8, 128))], axis=0))
    return jnp.concatenate(blocks, axis=1)


def store_blocks(ref, first, most, last):
    for i in range(GROUP):
        lanes = slice(128 * i, 128 * i + 128)
        ref[pl.ds(first + i, 24, stride=64), :] = most[:, lanes]
        ref[pl.ds(24 * 64 + first + i, 1), :] = last[:, lanes]


def lane_rows(ref, first, count):
    return jnp.concatenate([ref[pl.ds(first + i, 1), :] for i in range(count)], axis=1)


def translate(w_cat, value, octant):
    product = dot(w_cat, stacked(value, 0))
    total = product[0:24]
    for o in range(1, 8):
        total = jnp.where(octant == o, product[24 * o : 24 * o + 24], total)
    chosen = octant == lax.broadcasted_iota(jnp.int32, (8, 1), 0)
    last = jnp.sum(jnp.where(chosen, product[192:200], 0.0), axis=0, keepdims=True)
    return total, last


GROUP = 8
BATCH = 5


def head_kernel(leaf_ref, order_ref, octant_ref, op_ref, out_ref, ws):
    w_cat = load_operators(op_ref, ws)
    degree = degree_column()

    def group(g, carry):
        b = g * GROUP
        kept = jnp.where(degree <= lane_rows(order_ref, b, GROUP), load_blocks(leaf_ref, b), 0.0)
        store_blocks(out_ref, b, *translate(w_cat, kept, lane_rows(octant_ref, b, GROUP)))
        return carry

    lax.fori_loop(0, 64 // GROUP, group, 0)


def z_forward_kernel(ms, table_ref, _0, _1, out_ref):
    me = lax.axis_index("narrow")
    table = table_ref[me]
    for m in range(16):
        out_ref[m * 128 + 120 : m * 128 + 128, :] = jnp.zeros((8, 128), F32)

    def coefficients(g, carry):
        first = g * BATCH
        rows = pl.ds(pl.multiple_of(first * 64, 64), 64 * BATCH)
        pieces = []
        for part in split(ms[rows, :]):
            halves_ = [part[64 * i : 64 * i + 64, 64 * y2 : 64 * y2 + 64] for i in range(BATCH) for y2 in range(2)]
            pieces.append(jnp.concatenate(halves_, axis=0))
        high, low = pieces
        result = dot(table, jnp.concatenate([high, high, low], axis=1), ((1,), (1,)))
        for i in range(BATCH):
            for p in range(2):
                for t in range(SLOTS):
                    row = 40 * p + 8 * t
                    value = result[row : row + 8, 128 * i : 128 * i + 128]
                    out_ref[pl.ds(p * 128 + t * NC + first + i, 8, stride=256), :] = value
        return carry

    lax.fori_loop(0, NC // BATCH, coefficients, 0)


def y_forward_kernel(*refs):
    *parts, table_ref, _, out_ref = refs
    total = parts[0][...]
    for part in parts[1:]:
        total = total + part[0:256, :]
    total = jnp.concatenate([total[0:128], total[128:256]], axis=1)
    out_ref[...] = dot(table_ref[...], stacked(total, 1), ((1,), (1,)))


def pack_kernel(k_ref, even_ref, odd_ref, rows):
    for k2, send_ref in enumerate((even_ref, odd_ref)):
        rows[...] = jnp.concatenate([k_ref[0, :, k2].reshape(72, GRID), k_ref[1, :, k2].reshape(72, GRID)], axis=1)
        send_ref[...] = jnp.zeros_like(send_ref)
        for i in range(3):
            send_ref[9 * i : 9 * i + 9, :] = rows[pl.ds(5 + i, 9, stride=8), :]


def prepare_kernel(k_ref, r0_ref, r1_ref, coupling_ref, expand_ref, rows_ref, lanes_ref, mask_ref, flip_ref, k_out, c_out):
    exact = lax.Precision.HIGHEST
    for part in range(2):
        for k2 in range(2):
            own = k_ref[part, :, k2].reshape(72, GRID)
            mirror = (r0_ref, r1_ref)[k2][:, 64 * part : 64 * part + 64]
            mirror = dot(mirror, flip_ref[...], precision=exact)
            if part == 1:
                mirror = -mirror
            both = jnp.concatenate([own, mirror], axis=0).T
            k_out[part, k2 * 64 : k2 * 64 + 64, :] = dot(both, expand_ref[...], precision=exact)
    spread = dot(coupling_ref[...], lanes_ref[...], ((0,), (0,)), precision=exact)
    spread = dot(rows_ref[...], spread, precision=exact) * mask_ref[...]
    high, low = split(spread)
    c_out[...] = jnp.concatenate([high, low, high], axis=0)


def middle_kernel(a_ref, forward_ref, c_ref, k_ref, inverse_ref, out_ref):
    freq = dot(forward_ref[...], stacked(a_ref[...], 0))
    terms = dot(stacked(freq, 1), c_ref[...])
    pieces = []
    for k2 in range(2):
        real = jnp.zeros((64, 128), F32)
        imag = jnp.zeros((64, 128), F32)
        for s in range(ORDER + 1):
            lanes = slice(128 * s, 128 * s + 128)
            tr = terms[k2 * 128 : k2 * 128 + 64, lanes]
            ti = terms[k2 * 128 + 64 : k2 * 128 + 128, lanes]
            kr = k_ref[0, k2 * 64 : k2 * 64 + 64, lanes]
            ki = k_ref[1, k2 * 64 : k2 * 64 + 64, lanes]
            real = real + kr * tr - ki * ti
            imag = imag + kr * ti + ki * tr
        pieces += [real, imag]
    field = jnp.concatenate(pieces, axis=0)
    out_ref[...] = dot(inverse_ref[...], stacked(field, 0))


def y_inverse_kernel(a_ref, table_ref, out_ref):
    result = dot(stacked(a_ref[...].T, 1), table_ref[...])
    out_ref[0:128, :] = result[:, 0:128]
    out_ref[128:256, :] = result[:, 128:256]


def z_inverse_kernel(*refs):
    parts = refs[0:8]
    table_ref, ls, fs = refs[8:]
    row = 0
    for part in parts:
        rows = part.shape[0]
        fs[row : row + rows, :] = part[...]
        row += rows
    me = lax.axis_index("narrow")
    table = table_ref[me]

    def coefficients(g, carry):
        first = g * BATCH
        freqs = []
        for i in range(BATCH):
            rows = []
            for p in range(2):
                for t in range(SLOTS):
                    rows.append(fs[pl.ds(p * 128 + t * NC + first + i, 8, stride=256), :])
            freqs.append(jnp.concatenate(rows, axis=0))
        result = dot(table, stacked(jnp.concatenate(freqs, axis=1), 0))
        for i in range(BATCH):
            plane = result[:, 128 * i : 128 * i + 128].T
            rows = pl.ds(pl.multiple_of((first + i) * 64, 64), 64)
            ls[rows, :] = jnp.concatenate([plane[0:64], plane[64:128]], axis=1)
        return carry

    lax.fori_loop(0, NC // BATCH, coefficients, 0)


def tail_kernel(local_ref, octant_ref, op_ref, out_ref, ws):
    w_cat = load_operators(op_ref, ws)

    def group(g, carry):
        b = g * GROUP
        store_blocks(out_ref, b, *translate(w_cat, load_blocks(local_ref, b), lane_rows(octant_ref, b, GROUP)))
        return carry

    lax.fori_loop(0, 64 // GROUP, group, 0)


def call(kernel, out_shape, scratch=(), in_specs=None):
    args = {}
    if in_specs is not None:
        args["in_specs"] = in_specs
    return pl.pallas_call(
        kernel,
        out_shape=out_shape,
        scratch_shapes=list(scratch),
        compiler_params=pltpu.CompilerParams(vmem_limit_bytes=VMEM_LIMIT),
        **args,
    )


def shape(*dims, dtype=F32):
    return jax.ShapeDtypeStruct(dims, dtype)


Z_FORWARD, Z_INVERSE = z_tables()
Y_FORWARD, Y_INVERSE = y_tables()
X_FORWARD, X_INVERSE = x_tables()
EXPAND, ROWS, LANES, MASK, FLIP = expand_tables()


def block_rows(array):
    lead = array.shape[:-2]
    array = array.reshape(lead + (2, 32, 128))
    array = jnp.swapaxes(array, -3, -2)
    return array.reshape(-1, 128)


def shift(array, step):
    return lax.ppermute(array, "narrow", [(n, stepped(n, step, 1)) for n in range(8)])


def shards(leaf_multipoles, leaf_order, subtree_octant, m2m_operators, coupling, kernel_spectrum, l2l_operators):
    leaves = block_rows(leaf_multipoles[0])
    orders = block_rows(leaf_order[0])
    octants = block_rows(subtree_octant[0])
    m2m = jnp.swapaxes(m2m_operators, 0, 1).reshape(NC * 8, NC)
    l2l = jnp.swapaxes(l2l_operators, 0, 1).reshape(NC * 8, NC)
    kernel = kernel_spectrum.transpose(0, 1, 3, 4, 2)

    to_even = [(w * 8 + n, ((32 - w) % 32) * 8 + 7 - n) for w in range(32) for n in range(8)]
    to_odd = [(w * 8 + n, (31 - w) * 8 + 7 - n) for w in range(32) for n in range(8)]
    even, odd = call(pack_kernel, (shape(32, 128), shape(32, 128)), [pltpu.VMEM((72, 128), F32)])(kernel)
    mirror0 = lax.ppermute(even, ("wide", "narrow"), to_even)
    mirror1 = lax.ppermute(odd, ("wide", "narrow"), to_odd)

    moments = call(head_kernel, shape(NC * 64, 128), [pltpu.VMEM((256, 128), F32)])(leaves, orders, octants, m2m)
    whole = pl.BlockSpec(memory_space=pltpu.VMEM)
    anywhere = pl.BlockSpec(memory_space=pl.ANY)
    chunks = call(z_forward_kernel, shape(2048, 128), (), [whole] * 2 + [anywhere] * 2)(
        moments, jnp.asarray(Z_FORWARD), mirror0, mirror1
    )
    chunks = chunks.reshape(8, 256, 128)
    far = shift(chunks[1] + shift(chunks[5], ACROSS), FAR)
    across = chunks[4] + shift(chunks[6], ABOVE) + shift(chunks[7], BELOW)
    received = [chunks[0], far, shift(chunks[2], ABOVE), shift(chunks[3], BELOW), shift(across, ACROSS)]

    kernels, couplings = call(prepare_kernel, (shape(2, 128, 640), shape(384, 640, dtype=BF)))(
        kernel, mirror0, mirror1, coupling,
        jnp.asarray(EXPAND), jnp.asarray(ROWS), jnp.asarray(LANES), jnp.asarray(MASK), jnp.asarray(FLIP),
    )

    along = call(y_forward_kernel, shape(256, 128), (), [whole] * 6 + [anywhere])(
        *received, jnp.asarray(Y_FORWARD), kernels
    )
    along = lax.all_to_all(along.reshape(32, 8, 128), "wide", split_axis=0, concat_axis=0, tiled=True)
    along = call(middle_kernel, shape(256, 128))(
        along.reshape(256, 128), jnp.asarray(X_FORWARD), couplings, kernels, jnp.asarray(X_INVERSE)
    )
    along = lax.all_to_all(along.reshape(32, 8, 128), "wide", split_axis=0, concat_axis=0, tiled=True)
    plane = call(y_inverse_kernel, shape(256, 128))(along.reshape(256, 128), jnp.asarray(Y_INVERSE))

    other = shift(plane, ACROSS)
    far = shift(plane, FAR)
    above, below = shift(plane, ABOVE), shift(plane, BELOW)
    far_other, above_other, below_other = shift(far, ACROSS), shift(other, ABOVE), shift(other, BELOW)
    planes = [plane, far, above, below, other, far_other, above_other, below_other]
    local = call(z_inverse_kernel, shape(NC * 64, 128), [pltpu.VMEM((2048, 128), F32)])(*planes, jnp.asarray(Z_INVERSE))
    children = call(tail_kernel, shape(NC * 64, 128), [pltpu.VMEM((256, 128), F32)])(local, octants, l2l)
    children = children.reshape(NC, 32, 2, 128).swapaxes(1, 2)
    return children.reshape(1, NC, 2, 4096)


def solution(mesh):
    return jax.shard_map(
        shards,
        mesh=mesh,
        in_specs=(
            P("narrow", None, "wide", None),
            P("narrow", "wide", None),
            P("narrow", "wide", None),
            P(),
            P(),
            P(None, None, None, "wide", "narrow"),
            P(),
        ),
        out_specs=P("narrow", None, "wide", None),
        check_vma=False,
    )
```

```python
import numpy as np
import ml_dtypes

import jax
import jax.numpy as jnp
from jax import lax
from jax.experimental import pallas as pl
from jax.experimental.pallas import tpu as pltpu
from jax.sharding import PartitionSpec as P

ORDER = 4
GRID = 64
NC = 25
SLOTS = 5
BF = jnp.bfloat16
F32 = jnp.float32
VMEM_LIMIT = 48 * 1024 * 1024

FAR, ABOVE, BELOW, ACROSS = (2, 0), (1, 0), (-1, 0), (0, 1)
GATHER_STEPS = ((0, 0), FAR, ABOVE, BELOW, ACROSS, (2, 1), (1, 1), (-1, 1))
SUM_PARTNERS = (0, 1, 4, 5, 6, 7, 2, 3)

DEGREE = np.array([n for n in range(ORDER + 1) for _ in range(2 * n + 1)])


def halves(table):
    high = table.astype(ml_dtypes.bfloat16)
    low = (table - high.astype(np.float64)).astype(ml_dtypes.bfloat16)
    return high, low


def stack_left(table):
    high, low = halves(table)
    return np.concatenate([high, low, high], axis=1)


def stack_right(table):
    high, low = halves(table)
    return np.concatenate([high, low, high], axis=0)


def wave(a, b):
    angle = 2.0 * np.pi * ((a * b) % GRID) / GRID
    return np.cos(angle), np.sin(angle)


def complex_table(cosine, sine, sign):
    return np.stack([np.stack([cosine, -sign * sine]), np.stack([sign * sine, cosine])])


def stepped(n, step, sign):
    return (n // 2 + sign * step[0]) % 4 * 2 + (n + step[1]) % 2


def z_tables():
    z = np.arange(GRID)
    forward, inverse = [], []
    for n in range(8):
        tables = []
        towards = [n ^ partner for partner in SUM_PARTNERS]
        origins = [stepped(n, step, -1) for step in GATHER_STEPS]
        for devices in (towards, origins):
            rows = [8 * device + t for t in range(SLOTS) for device in devices]
            cosine, sine = wave(np.array(rows)[:, None], z[None, :])
            tables.append(np.concatenate([cosine, -sine], axis=0))
        forward.append(stack_left(tables[0]))
        inverse.append(stack_left(tables[1].T / GRID))
    return np.stack(forward), np.stack(inverse)


def y_tables():
    ky = np.arange(GRID)

    def place(table):
        table = table.reshape(2, 2, 2, 32, 2, 32, 2)
        table = table.transpose(3, 0, 4, 1, 2, 6, 5)
        full = np.zeros((32, 2, 2, 2, 2, 2, 2, 32, 2))
        for xl in range(2):
            full[:, :, xl, :, :, :, :, :, xl] = table
        return full

    waves = [wave(sign * ky[:, None], ky[None, :]) for sign in (1, -1)]
    forward = np.stack([complex_table(*w, -1) for w in waves])
    back = np.stack([complex_table(*w, 1).transpose(1, 0, 2, 3) for w in waves]) / GRID
    forward = place(forward).reshape(512, 256)
    inverse = place(back).reshape(512, 256)
    return stack_left(forward), stack_right(inverse)


def x_tables():
    kx = np.arange(GRID)
    cosine, sine = wave(kx[:, None], kx[None, :])

    def place(table):
        table = table.reshape(2, 2, GRID, 32, 2).transpose(0, 2, 3, 4, 1)
        full = np.zeros((2, 2, GRID, 32, 2, 2, 2))
        for k2 in range(2):
            full[k2, :, :, :, :, k2, :] = table
        return full.reshape(256, 256)

    forward = place(complex_table(cosine, sine, -1))
    back = complex_table(cosine, sine, 1) / GRID
    inverse = place(back.transpose(1, 0, 2, 3)).T
    return stack_left(forward), stack_left(inverse)


def expand_tables():
    own = np.zeros((72, 640), np.float32)
    mirror = np.zeros((32, 640), np.float32)
    rows = np.zeros((128, NC), np.float32)
    lanes = np.zeros((NC, 640), np.float32)
    mask = np.zeros((128, 640), np.float32)
    for t in range(SLOTS):
        for c in range(NC):
            rows[t * NC + c, c] = 1
            for s in range(ORDER + 1):
                lane = s * 128 + t * NC + c
                lanes[c, lane] = 1
                d = DEGREE[c] + s
                own[d * 8 + t, lane] = 1
                if 1 <= t <= 3:
                    mirror[(3 - t) * 9 + d, lane] = 1
                for j in range(NC):
                    if DEGREE[j] == s:
                        mask[t * NC + j, lane] = 1
    flip = np.zeros((GRID, GRID), np.float32)
    for k in range(GRID):
        flip[(-k) % GRID, k] = 1
    table = np.zeros((400, 640), ml_dtypes.bfloat16)
    table[0:72], table[80:112], table[112:137], table[144:272] = own, mirror, lanes, mask
    table[272:400, 0:NC], table[272:336, 128:192] = rows, flip
    return table


def split(value):
    high = value.astype(BF)
    low = (value - high.astype(F32)).astype(BF)
    return high, low


def stacked(value, axis):
    high, low = split(value)
    return jnp.concatenate([high, high, low], axis=axis)


def dot(a, b, dims=((1,), (0,)), precision=None):
    return lax.dot_general(a, b, (dims, ((), ())), precision=precision, preferred_element_type=F32)


def degree_column():
    row = lax.broadcasted_iota(jnp.int32, (32, 1), 0)
    one = lambda bound: (row >= bound).astype(jnp.int32)
    return one(1) + one(4) + one(9) + one(16) + 90 * one(25)


def load_operators(op_ref, w_ref):
    w_ref[...] = jnp.zeros_like(w_ref)
    w_ref[0:200, 0:NC] = op_ref[...]
    return operator_rows(w_ref, 0)


def operator_rows(ref, first):
    rows = [ref[pl.ds(first + octant, 24, stride=8), :] for octant in range(8)] + [ref[first + 192 : first + 200, :]]
    high, low = split(jnp.concatenate(rows, axis=0)[:, 0:32])
    return jnp.concatenate([high, low, high], axis=1)


def load_blocks(ref, first):
    blocks = []
    for i in range(GROUP):
        last = ref[pl.ds(24 * 64 + first + i, 1), :]
        blocks.append(jnp.concatenate([ref[pl.ds(first + i, 24, stride=64), :], jnp.broadcast_to(last, (8, 128))], axis=0))
    return jnp.concatenate(blocks, axis=1)


def store_blocks(ref, first, most, last):
    for i in range(GROUP):
        lanes = slice(128 * i, 128 * i + 128)
        ref[pl.ds(first + i, 24, stride=64), :] = most[:, lanes]
        ref[pl.ds(24 * 64 + first + i, 1), :] = last[:, lanes]


def lane_rows(ref, first, count):
    return jnp.concatenate([ref[pl.ds(first + i, 1), :] for i in range(count)], axis=1)


def translate(w_cat, value, octant):
    product = dot(w_cat, stacked(value, 0))
    total = product[0:24]
    for o in range(1, 8):
        total = jnp.where(octant == o, product[24 * o : 24 * o + 24], total)
    chosen = octant == lax.broadcasted_iota(jnp.int32, (8, 1), 0)
    last = jnp.sum(jnp.where(chosen, product[192:200], 0.0), axis=0, keepdims=True)
    return total, last


GROUP = 8
BATCH = 5


def head_kernel(leaf_ref, aux_ref, out_ref):
    w_cat = operator_rows(aux_ref, 128)
    degree = degree_column().astype(F32)

    def group(g, carry):
        b = g * GROUP
        kept = jnp.where(degree <= lane_rows(aux_ref, b, GROUP), load_blocks(leaf_ref, b), 0.0)
        octant = lane_rows(aux_ref, 64 + b, GROUP).astype(jnp.int32)
        store_blocks(out_ref, b, *translate(w_cat, kept, octant))
        return carry

    lax.fori_loop(0, 64 // GROUP, group, 0)


def z_forward_kernel(ms, table_ref, out_ref):
    me = lax.axis_index("narrow")
    table = table_ref[me]
    for m in range(16):
        out_ref[m * 128 + 120 : m * 128 + 128, :] = jnp.zeros((8, 128), F32)

    def coefficients(g, carry):
        first = g * BATCH
        rows = pl.ds(pl.multiple_of(first * 64, 64), 64 * BATCH)
        pieces = []
        for part in split(ms[rows, :]):
            halves_ = [part[64 * i : 64 * i + 64, 64 * y2 : 64 * y2 + 64] for i in range(BATCH) for y2 in range(2)]
            pieces.append(jnp.concatenate(halves_, axis=0))
        high, low = pieces
        result = dot(table, jnp.concatenate([high, high, low], axis=1), ((1,), (1,)))
        for i in range(BATCH):
            for p in range(2):
                for t in range(SLOTS):
                    row = 40 * p + 8 * t
                    value = result[row : row + 8, 128 * i : 128 * i + 128]
                    out_ref[pl.ds(p * 128 + t * NC + first + i, 8, stride=256), :] = value
        return carry

    lax.fori_loop(0, NC // BATCH, coefficients, 0)


def meet_kernel(here_ref, near_ref, _0, _1, _2, own_ref, across_ref):
    own_ref[...] = here_ref[0:256, :] + near_ref[0:256, :]
    across_ref[...] = here_ref[256:512, :] + near_ref[256:512, :]


def y_forward_kernel(*refs):
    *parts, table_ref, _, out_ref = refs
    total = parts[0][...]
    for part in parts[1:]:
        total = total + part[0:256, :]
    total = jnp.concatenate([total[0:128], total[128:256]], axis=1)
    out_ref[...] = dot(table_ref[...], stacked(total, 1), ((1,), (1,)))


def pack_kernel(k_ref, send_ref, rows):
    send_ref[...] = jnp.zeros_like(send_ref)
    for k2 in range(2):
        rows[...] = jnp.concatenate([k_ref[0, :, k2].reshape(72, GRID), k_ref[1, :, k2].reshape(72, GRID)], axis=1)
        for i in range(3):
            first = 32 * k2 + 9 * i
            send_ref[first : first + 9, :] = rows[pl.ds(5 + i, 9, stride=8), :]


def prepare_kernel(k_ref, mirror_ref, coupling_ref, table_ref, k_out, c_out):
    exact = lax.Precision.HIGHEST
    own_table = table_ref[0:80, :].astype(F32)[0:72]
    other_table = table_ref[80:112, :].astype(F32)
    lanes = table_ref[112:144, :].astype(F32)[0:NC]
    mask = table_ref[144:272, :].astype(F32)
    rest = table_ref[272:400, 0:256].astype(F32)
    flip = rest[0:64, 128:192]
    for part in range(2):
        for k2 in range(2):
            rows = slice(k2 * 64, k2 * 64 + 64)
            own = k_ref[part, :, k2].reshape(72, GRID).T
            k_out[0, part, rows, :] = dot(own, own_table, precision=exact)
            mirror = mirror_ref[32 * k2 : 32 * k2 + 32, 64 * part : 64 * part + 64]
            mirror = dot(mirror, flip, precision=exact).T
            if part == 1:
                mirror = -mirror
            k_out[1, part, rows, :] = dot(mirror, other_table, precision=exact)
    spread = dot(coupling_ref[...], lanes, ((0,), (0,)), precision=exact)
    spread = dot(rest[:, 0:NC], spread, precision=exact) * mask
    high, low = split(spread)
    c_out[...] = jnp.concatenate([high, low, high], axis=0)


def middle_kernel(a_ref, forward_ref, c_ref, k_ref, inverse_ref, out_ref):
    value = jnp.concatenate([a_ref[:, sign].reshape(256, 128) for sign in range(2)], axis=1)
    freq = dot(forward_ref[...], stacked(value, 0))
    freq = jnp.concatenate([freq[:, 0:128], freq[:, 128:256]], axis=0)
    terms = dot(stacked(freq, 1), c_ref[...])
    fields = []
    for sign in range(2):
        pieces = []
        for k2 in range(2):
            real = jnp.zeros((64, 128), F32)
            imag = jnp.zeros((64, 128), F32)
            row = sign * 256 + k2 * 128
            for s in range(ORDER + 1):
                lanes = slice(128 * s, 128 * s + 128)
                tr = terms[row : row + 64, lanes]
                ti = terms[row + 64 : row + 128, lanes]
                kr = k_ref[sign, 0, k2 * 64 : k2 * 64 + 64, lanes]
                ki = k_ref[sign, 1, k2 * 64 : k2 * 64 + 64, lanes]
                real = real + kr * tr - ki * ti
                imag = imag + kr * ti + ki * tr
            pieces += [real, imag]
        fields.append(jnp.concatenate(pieces, axis=0))
    result = dot(inverse_ref[...], stacked(jnp.concatenate(fields, axis=1), 0))
    for sign in range(2):
        out_ref[:, sign] = result[:, 128 * sign : 128 * sign + 128].reshape(32, 8, 128)


def y_inverse_kernel(a_ref, table_ref, out_ref):
    result = dot(stacked(a_ref[...].T, 1), table_ref[...])
    out_ref[0:128, :] = result[:, 0:128]
    out_ref[128:256, :] = result[:, 128:256]


def z_inverse_kernel(*refs):
    parts = refs[0:8]
    table_ref, ls, fs = refs[8:]
    row = 0
    for part in parts:
        rows = part.shape[0]
        fs[row : row + rows, :] = part[...]
        row += rows
    me = lax.axis_index("narrow")
    table = table_ref[me]

    def coefficients(g, carry):
        first = g * BATCH
        freqs = []
        for i in range(BATCH):
            rows = []
            for p in range(2):
                for t in range(SLOTS):
                    rows.append(fs[pl.ds(p * 128 + t * NC + first + i, 8, stride=256), :])
            freqs.append(jnp.concatenate(rows, axis=0))
        result = dot(table, stacked(jnp.concatenate(freqs, axis=1), 0))
        for i in range(BATCH):
            plane = result[:, 128 * i : 128 * i + 128].T
            rows = pl.ds(pl.multiple_of((first + i) * 64, 64), 64)
            ls[rows, :] = jnp.concatenate([plane[0:64], plane[64:128]], axis=1)
        return carry

    lax.fori_loop(0, NC // BATCH, coefficients, 0)


def tail_kernel(local_ref, octant_ref, op_ref, out_ref, ws):
    w_cat = load_operators(op_ref, ws)

    def group(g, carry):
        b = g * GROUP
        store_blocks(out_ref, b, *translate(w_cat, load_blocks(local_ref, b), lane_rows(octant_ref, b, GROUP)))
        return carry

    lax.fori_loop(0, 64 // GROUP, group, 0)


def call(kernel, out_shape, scratch=(), in_specs=None):
    args = {}
    if in_specs is not None:
        args["in_specs"] = in_specs
    return pl.pallas_call(
        kernel,
        out_shape=out_shape,
        scratch_shapes=list(scratch),
        compiler_params=pltpu.CompilerParams(vmem_limit_bytes=VMEM_LIMIT),
        **args,
    )


def shape(*dims, dtype=F32):
    return jax.ShapeDtypeStruct(dims, dtype)


Z_FORWARD, Z_INVERSE = z_tables()
Y_FORWARD, Y_INVERSE = y_tables()
X_FORWARD, X_INVERSE = x_tables()
EXPAND = expand_tables()


def block_rows(array):
    lead = array.shape[:-2]
    array = array.reshape(lead + (2, 32, 128))
    array = jnp.swapaxes(array, -3, -2)
    return array.reshape(-1, 128)


def swap(array, partner):
    return lax.ppermute(array, "narrow", [(n, n ^ partner) for n in range(8)])


def shift(array, step):
    return lax.ppermute(array, "narrow", [(n, stepped(n, step, 1)) for n in range(8)])


def shards(leaf_multipoles, leaf_order, subtree_octant, m2m_operators, coupling, kernel_spectrum, l2l_operators):
    leaves = block_rows(leaf_multipoles[0])
    orders = block_rows(leaf_order[0])
    octants = block_rows(subtree_octant[0])
    m2m = jnp.swapaxes(m2m_operators, 0, 1).reshape(NC * 8, NC)
    l2l = jnp.swapaxes(l2l_operators, 0, 1).reshape(NC * 8, NC)
    kernel = kernel_spectrum.transpose(0, 1, 3, 4, 2)

    packed = call(pack_kernel, shape(64, 128), [pltpu.VMEM((72, 128), F32)])(kernel)
    mirror = lax.ppermute(packed, "narrow", [(n, 7 - n) for n in range(8)])
    aux = [orders.astype(F32), octants.astype(F32), jnp.pad(m2m, ((0, 0), (0, 128 - NC)))]
    moments = call(head_kernel, shape(NC * 64, 128))(leaves, jnp.concatenate(aux, axis=0))
    whole = pl.BlockSpec(memory_space=pltpu.VMEM)
    anywhere = pl.BlockSpec(memory_space=pl.ANY)
    chunks = call(z_forward_kernel, shape(2048, 128))(moments, jnp.asarray(Z_FORWARD))
    chunks = chunks.reshape(8, 256, 128)
    far = chunks[2] + swap(chunks[3], 1)
    mid = chunks[4] + swap(chunks[5], 1)
    near = swap(chunks[6:8].reshape(512, 128), 2)
    own, across = call(meet_kernel, (shape(256, 128), shape(256, 128)), (), [whole] * 2 + [anywhere] * 3)(
        chunks[0:2].reshape(512, 128), near, far, mid, mirror
    )
    received = [own, swap(far, 4), swap(mid, 6), swap(across, 1)]

    kernels, couplings = call(prepare_kernel, (shape(2, 2, 128, 640), shape(384, 640, dtype=BF)))(
        kernel, mirror, coupling, jnp.asarray(EXPAND)
    )

    along = call(y_forward_kernel, shape(512, 128), (), [whole] * 5 + [anywhere])(*received, jnp.asarray(Y_FORWARD), kernels)
    along = lax.all_to_all(along.reshape(32, 16, 128), "wide", split_axis=0, concat_axis=0, tiled=True)
    along = call(middle_kernel, shape(32, 2, 8, 128))(
        along.reshape(32, 2, 8, 128), jnp.asarray(X_FORWARD), couplings, kernels, jnp.asarray(X_INVERSE)
    )
    along = lax.all_to_all(along.reshape(32, 16, 128), "wide", split_axis=0, concat_axis=0, tiled=True)
    plane = call(y_inverse_kernel, shape(256, 128))(along.reshape(512, 128), jnp.asarray(Y_INVERSE))

    other = shift(plane, ACROSS)
    far = shift(plane, FAR)
    above, below = shift(plane, ABOVE), shift(plane, BELOW)
    far_other, above_other, below_other = shift(far, ACROSS), shift(other, ABOVE), shift(other, BELOW)
    planes = [plane, far, above, below, other, far_other, above_other, below_other]
    local = call(z_inverse_kernel, shape(NC * 64, 128), [pltpu.VMEM((2048, 128), F32)])(*planes, jnp.asarray(Z_INVERSE))
    children = call(tail_kernel, shape(NC * 64, 128), [pltpu.VMEM((256, 128), F32)])(local, octants, l2l)
    children = children.reshape(NC, 32, 2, 128).swapaxes(1, 2)
    return children.reshape(1, NC, 2, 4096)


def solution(mesh):
    return jax.shard_map(
        shards,
        mesh=mesh,
        in_specs=(
            P("narrow", None, "wide", None),
            P("narrow", "wide", None),
            P("narrow", "wide", None),
            P(),
            P(),
            P(None, None, None, "wide", "narrow"),
            P(),
        ),
        out_specs=P("narrow", None, "wide", None),
        check_vma=False,
    )
```

```python
import numpy as np
import ml_dtypes

import jax
import jax.numpy as jnp
from jax import lax
from jax.experimental import pallas as pl
from jax.experimental.pallas import tpu as pltpu
from jax.sharding import PartitionSpec as P

ORDER = 4
GRID = 64
NC = 25
SLOTS = 5
BF = jnp.bfloat16
F32 = jnp.float32
VMEM_LIMIT = 48 * 1024 * 1024

FAR, ABOVE, BELOW, ACROSS = (2, 0), (1, 0), (-1, 0), (0, 1)
GATHER_STEPS = ((0, 0), FAR, ABOVE, BELOW, ACROSS, (2, 1), (1, 1), (-1, 1))
SUM_PARTNERS = (0, 1, 4, 5, 6, 7, 2, 3)

DEGREE = np.array([n for n in range(ORDER + 1) for _ in range(2 * n + 1)])


def halves(table):
    high = table.astype(ml_dtypes.bfloat16)
    low = (table - high.astype(np.float64)).astype(ml_dtypes.bfloat16)
    return high, low


def stack_left(table):
    high, low = halves(table)
    return np.concatenate([high, low, high], axis=1)


def stack_right(table):
    high, low = halves(table)
    return np.concatenate([high, low, high], axis=0)


def wave(a, b):
    angle = 2.0 * np.pi * ((a * b) % GRID) / GRID
    return np.cos(angle), np.sin(angle)


def complex_table(cosine, sine, sign):
    return np.stack([np.stack([cosine, -sign * sine]), np.stack([sign * sine, cosine])])


def stepped(n, step, sign):
    return (n // 2 + sign * step[0]) % 4 * 2 + (n + step[1]) % 2


def z_tables():
    z = np.arange(GRID)
    forward, inverse = [], []
    for n in range(8):
        tables = []
        towards = [n ^ partner for partner in SUM_PARTNERS]
        origins = [stepped(n, step, -1) for step in GATHER_STEPS]
        for devices in (towards, origins):
            rows = [8 * device + t for t in range(SLOTS) for device in devices]
            cosine, sine = wave(np.array(rows)[:, None], z[None, :])
            tables.append(np.concatenate([cosine, -sine], axis=0))
        forward.append(stack_left(tables[0]))
        inverse.append(stack_left(tables[1].T / GRID))
    return np.stack(forward), np.stack(inverse)


def y_tables():
    ky = np.arange(GRID)

    def place(table):
        table = table.reshape(2, 2, 2, 32, 2, 32, 2)
        table = table.transpose(3, 0, 4, 1, 2, 6, 5)
        full = np.zeros((32, 2, 2, 2, 2, 2, 2, 32, 2))
        for xl in range(2):
            full[:, :, xl, :, :, :, :, :, xl] = table
        return full

    waves = [wave(sign * ky[:, None], ky[None, :]) for sign in (1, -1)]
    forward = np.stack([complex_table(*w, -1) for w in waves])
    back = np.stack([complex_table(*w, 1).transpose(1, 0, 2, 3) for w in waves]) / GRID
    forward = place(forward).reshape(512, 256)
    inverse = place(back).reshape(512, 256)
    return stack_left(forward), stack_right(inverse)


def x_tables():
    kx = np.arange(GRID)
    cosine, sine = wave(kx[:, None], kx[None, :])

    def place(table):
        table = table.reshape(2, 2, GRID, 32, 2).transpose(0, 2, 3, 4, 1)
        full = np.zeros((2, 2, GRID, 32, 2, 2, 2))
        for k2 in range(2):
            full[k2, :, :, :, :, k2, :] = table
        return full.reshape(256, 256)

    forward = place(complex_table(cosine, sine, -1))
    back = complex_table(cosine, sine, 1) / GRID
    inverse = place(back.transpose(1, 0, 2, 3)).T
    return stack_left(forward), stack_left(inverse)


def expand_tables():
    own = np.zeros((72, 640), np.float32)
    mirror = np.zeros((32, 640), np.float32)
    rows = np.zeros((128, NC), np.float32)
    lanes = np.zeros((NC, 640), np.float32)
    mask = np.zeros((128, 640), np.float32)
    for t in range(SLOTS):
        for c in range(NC):
            rows[t * NC + c, c] = 1
            for s in range(ORDER + 1):
                lane = s * 128 + t * NC + c
                lanes[c, lane] = 1
                d = DEGREE[c] + s
                own[d * 8 + t, lane] = 1
                if 1 <= t <= 3:
                    mirror[(3 - t) * 9 + d, lane] = 1
                for j in range(NC):
                    if DEGREE[j] == s:
                        mask[t * NC + j, lane] = 1
    flip = np.zeros((GRID, GRID), np.float32)
    for k in range(GRID):
        flip[(-k) % GRID, k] = 1
    table = np.zeros((400, 640), ml_dtypes.bfloat16)
    table[0:72], table[80:112], table[112:137], table[144:272] = own, mirror, lanes, mask
    table[272:400, 0:NC], table[272:336, 128:192] = rows, flip
    return table


def split(value):
    high = value.astype(BF)
    low = (value - high.astype(F32)).astype(BF)
    return high, low


def stacked(value, axis):
    high, low = split(value)
    return jnp.concatenate([high, high, low], axis=axis)


def dot(a, b, dims=((1,), (0,)), precision=None):
    return lax.dot_general(a, b, (dims, ((), ())), precision=precision, preferred_element_type=F32)


def degree_column():
    row = lax.broadcasted_iota(jnp.int32, (32, 1), 0)
    one = lambda bound: (row >= bound).astype(jnp.int32)
    return one(1) + one(4) + one(9) + one(16) + 90 * one(25)


def load_operators(op_ref, w_ref):
    w_ref[...] = jnp.zeros_like(w_ref)
    w_ref[0:200, 0:NC] = op_ref[...]
    return operator_rows(w_ref, 0)


def operator_rows(ref, first):
    rows = [ref[pl.ds(first + octant, 24, stride=8), :] for octant in range(8)] + [ref[first + 192 : first + 200, :]]
    high, low = split(jnp.concatenate(rows, axis=0)[:, 0:32])
    return jnp.concatenate([high, low, high], axis=1)


def load_blocks(ref, first):
    blocks = []
    for i in range(GROUP):
        last = ref[pl.ds(24 * 64 + first + i, 1), :]
        blocks.append(jnp.concatenate([ref[pl.ds(first + i, 24, stride=64), :], jnp.broadcast_to(last, (8, 128))], axis=0))
    return jnp.concatenate(blocks, axis=1)


def store_blocks(ref, first, most, last):
    for i in range(GROUP):
        lanes = slice(128 * i, 128 * i + 128)
        ref[pl.ds(first + i, 24, stride=64), :] = most[:, lanes]
        ref[pl.ds(24 * 64 + first + i, 1), :] = last[:, lanes]


def lane_rows(ref, first, count):
    return jnp.concatenate([ref[pl.ds(first + i, 1), :] for i in range(count)], axis=1)


def translate(w_cat, value, octant):
    product = dot(w_cat, stacked(value, 0))
    total = product[0:24]
    for o in range(1, 8):
        total = jnp.where(octant == o, product[24 * o : 24 * o + 24], total)
    chosen = octant == lax.broadcasted_iota(jnp.int32, (8, 1), 0)
    last = jnp.sum(jnp.where(chosen, product[192:200], 0.0), axis=0, keepdims=True)
    return total, last


GROUP = 32
BATCH = 25


def head_kernel(leaf_ref, aux_ref, out_ref):
    w_cat = operator_rows(aux_ref, 128)
    degree = degree_column().astype(F32)

    def group(g, carry):
        b = g * GROUP
        kept = jnp.where(degree <= lane_rows(aux_ref, b, GROUP), load_blocks(leaf_ref, b), 0.0)
        octant = lane_rows(aux_ref, 64 + b, GROUP).astype(jnp.int32)
        store_blocks(out_ref, b, *translate(w_cat, kept, octant))
        return carry

    lax.fori_loop(0, 64 // GROUP, group, 0)


def z_forward_kernel(ms, table_ref, out_ref):
    me = lax.axis_index("narrow")
    table = table_ref[me]
    for m in range(16):
        out_ref[m * 128 + 120 : m * 128 + 128, :] = jnp.zeros((8, 128), F32)

    def coefficients(g, carry):
        first = g * BATCH
        rows = pl.ds(pl.multiple_of(first * 64, 64), 64 * BATCH)
        pieces = []
        for part in split(ms[rows, :]):
            halves_ = [part[64 * i : 64 * i + 64, 64 * y2 : 64 * y2 + 64] for i in range(BATCH) for y2 in range(2)]
            pieces.append(jnp.concatenate(halves_, axis=0))
        high, low = pieces
        result = dot(table, jnp.concatenate([high, high, low], axis=1), ((1,), (1,)))
        for i in range(BATCH):
            for p in range(2):
                for t in range(SLOTS):
                    row = 40 * p + 8 * t
                    value = result[row : row + 8, 128 * i : 128 * i + 128]
                    out_ref[pl.ds(p * 128 + t * NC + first + i, 8, stride=256), :] = value
        return carry

    lax.fori_loop(0, NC // BATCH, coefficients, 0)


def lift_kernel(far_ref, mid_ref, far_other, mid_other, far_out, mid_out):
    far_out[...] = far_ref[...] + far_other[...]
    mid_out[...] = mid_ref[...] + mid_other[...]


def meet_kernel(here_ref, near_ref, _0, _1, _2, own_ref, across_ref):
    own_ref[...] = here_ref[0:256, :] + near_ref[0:256, :]
    across_ref[...] = here_ref[256:512, :] + near_ref[256:512, :]


def y_forward_kernel(*refs):
    *parts, table_ref, _, out_ref = refs
    total = parts[0][...]
    for part in parts[1:]:
        total = total + part[0:256, :]
    total = jnp.concatenate([total[0:128], total[128:256]], axis=1)
    out_ref[...] = dot(table_ref[...], stacked(total, 1), ((1,), (1,)))


def pack_kernel(k_ref, send_ref, rows):
    send_ref[...] = jnp.zeros_like(send_ref)
    for k2 in range(2):
        rows[...] = jnp.concatenate([k_ref[0, :, k2].reshape(72, GRID), k_ref[1, :, k2].reshape(72, GRID)], axis=1)
        for i in range(3):
            first = 32 * k2 + 9 * i
            send_ref[first : first + 9, :] = rows[pl.ds(5 + i, 9, stride=8), :]


def spread(value, table):
    high, low = split(value)
    return dot(high, table) + dot(low, table)


def prepare_kernel(k_ref, mirror_ref, coupling_ref, table_ref, k_out, c_out):
    own_table = table_ref[0:80, :]
    other_table = table_ref[80:112, :]
    lanes = table_ref[112:144, :]
    mask = table_ref[144:272, :].astype(F32)
    rest = table_ref[272:400, 0:256].astype(F32)
    flip = rest[0:64, 128:192].astype(BF)
    rows = rest[:, 0:32].astype(BF)
    zeros = jnp.zeros((8, GRID), F32)
    for part in range(2):
        for k2 in range(2):
            place = slice(k2 * 64, k2 * 64 + 64)
            own = jnp.concatenate([k_ref[part, :, k2].reshape(72, GRID), zeros], axis=0).T
            k_out[0, part, place, :] = spread(own, own_table)
            mirror = mirror_ref[32 * k2 : 32 * k2 + 32, 64 * part : 64 * part + 64]
            mirror = spread(mirror, flip).T
            if part == 1:
                mirror = -mirror
            k_out[1, part, place, :] = spread(mirror, other_table)
    high, low = split(spread(coupling_ref[...].T, lanes))
    placed = (dot(rows, high) + dot(rows, low)) * mask
    high, low = split(placed)
    c_out[...] = jnp.concatenate([high, low, high], axis=0)


def middle_kernel(a_ref, forward_ref, c_ref, k_ref, inverse_ref, out_ref):
    value = jnp.concatenate([a_ref[:, sign].reshape(256, 128) for sign in range(2)], axis=1)
    freq = dot(forward_ref[...], stacked(value, 0))
    freq = jnp.concatenate([freq[:, 0:128], freq[:, 128:256]], axis=0)
    terms = dot(stacked(freq, 1), c_ref[...])
    fields = []
    for sign in range(2):
        pieces = []
        for k2 in range(2):
            real = jnp.zeros((64, 128), F32)
            imag = jnp.zeros((64, 128), F32)
            row = sign * 256 + k2 * 128
            for s in range(ORDER + 1):
                lanes = slice(128 * s, 128 * s + 128)
                tr = terms[row : row + 64, lanes]
                ti = terms[row + 64 : row + 128, lanes]
                kr = k_ref[sign, 0, k2 * 64 : k2 * 64 + 64, lanes]
                ki = k_ref[sign, 1, k2 * 64 : k2 * 64 + 64, lanes]
                real = real + kr * tr - ki * ti
                imag = imag + kr * ti + ki * tr
            pieces += [real, imag]
        fields.append(jnp.concatenate(pieces, axis=0))
    result = dot(inverse_ref[...], stacked(jnp.concatenate(fields, axis=1), 0))
    for sign in range(2):
        out_ref[:, sign] = result[:, 128 * sign : 128 * sign + 128].reshape(32, 8, 128)


def y_inverse_kernel(a_ref, table_ref, out_ref):
    result = dot(stacked(a_ref[...].T, 1), table_ref[...])
    out_ref[0:128, :] = result[:, 0:128]
    out_ref[128:256, :] = result[:, 128:256]


def z_inverse_kernel(*refs):
    parts = refs[0:8]
    table_ref, ls, fs = refs[8:]
    row = 0
    for part in parts:
        rows = part.shape[0]
        fs[row : row + rows, :] = part[...]
        row += rows
    me = lax.axis_index("narrow")
    table = table_ref[me]

    def coefficients(g, carry):
        first = g * BATCH
        freqs = []
        for i in range(BATCH):
            rows = []
            for p in range(2):
                for t in range(SLOTS):
                    rows.append(fs[pl.ds(p * 128 + t * NC + first + i, 8, stride=256), :])
            freqs.append(jnp.concatenate(rows, axis=0))
        result = dot(table, stacked(jnp.concatenate(freqs, axis=1), 0))
        for i in range(BATCH):
            plane = result[:, 128 * i : 128 * i + 128].T
            rows = pl.ds(pl.multiple_of((first + i) * 64, 64), 64)
            ls[rows, :] = jnp.concatenate([plane[0:64], plane[64:128]], axis=1)
        return carry

    lax.fori_loop(0, NC // BATCH, coefficients, 0)


def tail_kernel(local_ref, octant_ref, op_ref, out_ref, ws):
    w_cat = load_operators(op_ref, ws)

    def group(g, carry):
        b = g * GROUP
        store_blocks(out_ref, b, *translate(w_cat, load_blocks(local_ref, b), lane_rows(octant_ref, b, GROUP)))
        return carry

    lax.fori_loop(0, 64 // GROUP, group, 0)


def call(kernel, out_shape, scratch=(), in_specs=None):
    args = {}
    if in_specs is not None:
        args["in_specs"] = in_specs
    return pl.pallas_call(
        kernel,
        out_shape=out_shape,
        scratch_shapes=list(scratch),
        compiler_params=pltpu.CompilerParams(vmem_limit_bytes=VMEM_LIMIT),
        **args,
    )


def shape(*dims, dtype=F32):
    return jax.ShapeDtypeStruct(dims, dtype)


Z_FORWARD, Z_INVERSE = z_tables()
Y_FORWARD, Y_INVERSE = y_tables()
X_FORWARD, X_INVERSE = x_tables()
EXPAND = expand_tables()


def block_rows(array):
    lead = array.shape[:-2]
    array = array.reshape(lead + (2, 32, 128))
    array = jnp.swapaxes(array, -3, -2)
    return array.reshape(-1, 128)


def swap(array, partner):
    return lax.ppermute(array, "narrow", [(n, n ^ partner) for n in range(8)])


def shift(array, step):
    return lax.ppermute(array, "narrow", [(n, stepped(n, step, 1)) for n in range(8)])


def shards(leaf_multipoles, leaf_order, subtree_octant, m2m_operators, coupling, kernel_spectrum, l2l_operators):
    leaves = block_rows(leaf_multipoles[0])
    orders = block_rows(leaf_order[0])
    octants = block_rows(subtree_octant[0])
    m2m = jnp.swapaxes(m2m_operators, 0, 1).reshape(NC * 8, NC)
    l2l = jnp.swapaxes(l2l_operators, 0, 1).reshape(NC * 8, NC)
    kernel = kernel_spectrum.transpose(0, 1, 3, 4, 2)

    packed = call(pack_kernel, shape(64, 128), [pltpu.VMEM((72, 128), F32)])(kernel)
    mirror = lax.ppermute(packed, "narrow", [(n, 7 - n) for n in range(8)])
    aux = [orders.astype(F32), octants.astype(F32), jnp.pad(m2m, ((0, 0), (0, 128 - NC)))]
    moments = call(head_kernel, shape(NC * 64, 128))(leaves, jnp.concatenate(aux, axis=0))
    whole = pl.BlockSpec(memory_space=pltpu.VMEM)
    anywhere = pl.BlockSpec(memory_space=pl.ANY)
    chunks = call(z_forward_kernel, shape(2048, 128))(moments, jnp.asarray(Z_FORWARD))
    chunks = chunks.reshape(8, 256, 128)
    far, mid = call(lift_kernel, (shape(256, 128), shape(256, 128)))(
        chunks[2], chunks[4], swap(chunks[3], 1), swap(chunks[5], 1)
    )
    near = swap(chunks[6:8].reshape(512, 128), 2)
    own, across = call(meet_kernel, (shape(256, 128), shape(256, 128)), (), [whole] * 2 + [anywhere] * 3)(
        chunks[0:2].reshape(512, 128), near, far, mid, mirror
    )
    received = [own, swap(far, 4), swap(mid, 6), swap(across, 1)]

    kernels, couplings = call(prepare_kernel, (shape(2, 2, 128, 640), shape(384, 640, dtype=BF)))(
        kernel, mirror, jnp.pad(coupling, ((0, 32 - NC), (0, 32 - NC))), jnp.asarray(EXPAND)
    )

    along = call(y_forward_kernel, shape(512, 128), (), [whole] * 5 + [anywhere])(*received, jnp.asarray(Y_FORWARD), kernels)
    along = lax.all_to_all(along.reshape(32, 16, 128), "wide", split_axis=0, concat_axis=0, tiled=True)
    along = call(middle_kernel, shape(32, 2, 8, 128))(
        along.reshape(32, 2, 8, 128), jnp.asarray(X_FORWARD), couplings, kernels, jnp.asarray(X_INVERSE)
    )
    along = lax.all_to_all(along.reshape(32, 16, 128), "wide", split_axis=0, concat_axis=0, tiled=True)
    plane = call(y_inverse_kernel, shape(256, 128))(along.reshape(512, 128), jnp.asarray(Y_INVERSE))

    other = shift(plane, ACROSS)
    far = shift(plane, FAR)
    above, below = shift(plane, ABOVE), shift(plane, BELOW)
    far_other, above_other, below_other = shift(far, ACROSS), shift(other, ABOVE), shift(other, BELOW)
    planes = [plane, far, above, below, other, far_other, above_other, below_other]
    local = call(z_inverse_kernel, shape(NC * 64, 128), [pltpu.VMEM((2048, 128), F32)])(*planes, jnp.asarray(Z_INVERSE))
    children = call(tail_kernel, shape(NC * 64, 128), [pltpu.VMEM((256, 128), F32)])(local, octants, l2l)
    children = children.reshape(NC, 32, 2, 128).swapaxes(1, 2)
    return children.reshape(1, NC, 2, 4096)


def solution(mesh):
    return jax.shard_map(
        shards,
        mesh=mesh,
        in_specs=(
            P("narrow", None, "wide", None),
            P("narrow", "wide", None),
            P("narrow", "wide", None),
            P(),
            P(),
            P(None, None, None, "wide", "narrow"),
            P(),
        ),
        out_specs=P("narrow", None, "wide", None),
        check_vma=False,
    )
```

```python
import numpy as np
import ml_dtypes

import jax
import jax.numpy as jnp
from jax import lax
from jax.experimental import pallas as pl
from jax.experimental.pallas import tpu as pltpu
from jax.sharding import PartitionSpec as P

ORDER = 4
GRID = 64
NC = 25
SLOTS = 5
BF = jnp.bfloat16
F32 = jnp.float32
VMEM_LIMIT = 48 * 1024 * 1024

FAR, ABOVE, BELOW, ACROSS = (2, 0), (1, 0), (-1, 0), (0, 1)
GATHER_STEPS = ((0, 0), FAR, ABOVE, BELOW, ACROSS, (2, 1), (1, 1), (-1, 1))
SUM_PARTNERS = (0, 1, 4, 5, 6, 7, 2, 3)

DEGREE = np.array([n for n in range(ORDER + 1) for _ in range(2 * n + 1)])


def halves(table):
    high = table.astype(ml_dtypes.bfloat16)
    low = (table - high.astype(np.float64)).astype(ml_dtypes.bfloat16)
    return high, low


def stack_left(table):
    high, low = halves(table)
    return np.concatenate([high, low, high], axis=1)


def stack_right(table):
    high, low = halves(table)
    return np.concatenate([high, low, high], axis=0)


def wave(a, b):
    angle = 2.0 * np.pi * ((a * b) % GRID) / GRID
    return np.cos(angle), np.sin(angle)


def complex_table(cosine, sine, sign):
    return np.stack([np.stack([cosine, -sign * sine]), np.stack([sign * sine, cosine])])


def stepped(n, step, sign):
    return (n // 2 + sign * step[0]) % 4 * 2 + (n + step[1]) % 2


def z_tables():
    z = np.arange(GRID)
    forward, inverse = [], []
    for n in range(8):
        tables = []
        towards = [n ^ partner for partner in SUM_PARTNERS]
        origins = [stepped(n, step, -1) for step in GATHER_STEPS]
        for devices in (towards, origins):
            rows = [8 * device + t for t in range(SLOTS) for device in devices]
            cosine, sine = wave(np.array(rows)[:, None], z[None, :])
            tables.append(np.concatenate([cosine, -sine], axis=0))
        forward.append(stack_left(tables[0]))
        inverse.append(stack_left(tables[1].T / GRID))
    return np.stack(forward), np.stack(inverse)


def y_tables():
    ky = np.arange(GRID)

    def place(table):
        table = table.reshape(2, 2, 2, 32, 2, 32, 2)
        table = table.transpose(3, 0, 4, 1, 2, 6, 5)
        full = np.zeros((32, 2, 2, 2, 2, 2, 2, 32, 2))
        for xl in range(2):
            full[:, :, xl, :, :, :, :, :, xl] = table
        return full

    waves = [wave(sign * ky[:, None], ky[None, :]) for sign in (1, -1)]
    forward = np.stack([complex_table(*w, -1) for w in waves])
    back = np.stack([complex_table(*w, 1).transpose(1, 0, 2, 3) for w in waves]) / GRID
    forward = place(forward).reshape(512, 256)
    inverse = place(back).reshape(512, 256)
    return stack_left(forward), stack_right(inverse)


def x_tables():
    kx = np.arange(GRID)
    cosine, sine = wave(kx[:, None], kx[None, :])

    def place(table):
        table = table.reshape(2, 2, GRID, 32, 2).transpose(0, 2, 3, 4, 1)
        full = np.zeros((2, 2, GRID, 32, 2, 2, 2))
        for k2 in range(2):
            full[k2, :, :, :, :, k2, :] = table
        return full.reshape(256, 256)

    forward = place(complex_table(cosine, sine, -1))
    back = complex_table(cosine, sine, 1) / GRID
    inverse = place(back.transpose(1, 0, 2, 3)).T
    return stack_left(forward), stack_left(inverse)


def expand_tables():
    own = np.zeros((72, 640), np.float32)
    mirror = np.zeros((32, 640), np.float32)
    rows = np.zeros((128, NC), np.float32)
    lanes = np.zeros((NC, 640), np.float32)
    mask = np.zeros((128, 640), np.float32)
    for t in range(SLOTS):
        for c in range(NC):
            rows[t * NC + c, c] = 1
            for s in range(ORDER + 1):
                lane = s * 128 + t * NC + c
                lanes[c, lane] = 1
                d = DEGREE[c] + s
                own[d * 8 + t, lane] = 1
                if 1 <= t <= 3:
                    mirror[(3 - t) * 9 + d, lane] = 1
                for j in range(NC):
                    if DEGREE[j] == s:
                        mask[t * NC + j, lane] = 1
    flip = np.zeros((GRID, GRID), np.float32)
    for k in range(GRID):
        flip[(-k) % GRID, k] = 1
    table = np.zeros((400, 640), ml_dtypes.bfloat16)
    table[0:72], table[80:112], table[112:137], table[144:272] = own, mirror, lanes, mask
    table[272:400, 0:NC], table[272:336, 128:192] = rows, flip
    return table


def split(value):
    high = value.astype(BF)
    low = (value - high.astype(F32)).astype(BF)
    return high, low


def stacked(value, axis):
    high, low = split(value)
    return jnp.concatenate([high, high, low], axis=axis)


def dot(a, b, dims=((1,), (0,)), precision=None):
    return lax.dot_general(a, b, (dims, ((), ())), precision=precision, preferred_element_type=F32)


def degree_column():
    row = lax.broadcasted_iota(jnp.int32, (32, 1), 0)
    one = lambda bound: (row >= bound).astype(jnp.int32)
    return one(1) + one(4) + one(9) + one(16) + 90 * one(25)


def load_operators(op_ref, w_ref):
    w_ref[...] = jnp.zeros_like(w_ref)
    w_ref[0:200, 0:NC] = op_ref[...]
    return operator_rows(w_ref, 0)


def operator_rows(ref, first):
    rows = [ref[pl.ds(first + octant, 24, stride=8), :] for octant in range(8)] + [ref[first + 192 : first + 200, :]]
    high, low = split(jnp.concatenate(rows, axis=0)[:, 0:32])
    return jnp.concatenate([high, low, high], axis=1)


def load_blocks(ref, first):
    blocks = []
    for i in range(GROUP):
        last = ref[pl.ds(24 * 64 + first + i, 1), :]
        blocks.append(jnp.concatenate([ref[pl.ds(first + i, 24, stride=64), :], jnp.broadcast_to(last, (8, 128))], axis=0))
    return jnp.concatenate(blocks, axis=1)


def store_blocks(ref, first, most, last):
    for i in range(GROUP):
        lanes = slice(128 * i, 128 * i + 128)
        ref[pl.ds(first + i, 24, stride=64), :] = most[:, lanes]
        ref[pl.ds(24 * 64 + first + i, 1), :] = last[:, lanes]


def lane_rows(ref, first, count):
    return jnp.concatenate([ref[pl.ds(first + i, 1), :] for i in range(count)], axis=1)


def translate(w_cat, value, octant):
    product = dot(w_cat, stacked(value, 0))
    total = product[0:24]
    for o in range(1, 8):
        total = jnp.where(octant == o, product[24 * o : 24 * o + 24], total)
    chosen = octant == lax.broadcasted_iota(jnp.int32, (8, 1), 0)
    last = jnp.sum(jnp.where(chosen, product[192:200], 0.0), axis=0, keepdims=True)
    return total, last


GROUP = 64
BATCH = 25


def head_kernel(leaf_ref, aux_ref, out_ref):
    w_cat = operator_rows(aux_ref, 64)
    degree = degree_column()

    def group(g, carry):
        b = g * GROUP
        code = lane_rows(aux_ref, b, GROUP).astype(jnp.int32)
        kept = jnp.where(degree <= (code & 7), load_blocks(leaf_ref, b), 0.0)
        store_blocks(out_ref, b, *translate(w_cat, kept, code >> 3))
        return carry

    lax.fori_loop(0, 64 // GROUP, group, 0)


def z_forward_kernel(ms, table_ref, out_ref):
    me = lax.axis_index("narrow")
    table = table_ref[me]
    for m in range(16):
        out_ref[m * 128 + 120 : m * 128 + 128, :] = jnp.zeros((8, 128), F32)

    def coefficients(g, carry):
        first = g * BATCH
        rows = pl.ds(pl.multiple_of(first * 64, 64), 64 * BATCH)
        pieces = []
        for part in split(ms[rows, :]):
            halves_ = [part[64 * i : 64 * i + 64, 64 * y2 : 64 * y2 + 64] for i in range(BATCH) for y2 in range(2)]
            pieces.append(jnp.concatenate(halves_, axis=0))
        high, low = pieces
        result = dot(table, jnp.concatenate([high, high, low], axis=1), ((1,), (1,)))
        for i in range(BATCH):
            for p in range(2):
                for t in range(SLOTS):
                    row = 40 * p + 8 * t
                    value = result[row : row + 8, 128 * i : 128 * i + 128]
                    out_ref[pl.ds(p * 128 + t * NC + first + i, 8, stride=256), :] = value
        return carry

    lax.fori_loop(0, NC // BATCH, coefficients, 0)


def lift_kernel(far_ref, mid_ref, far_other, mid_other, far_out, mid_out):
    far_out[...] = far_ref[...] + far_other[...]
    mid_out[...] = mid_ref[...] + mid_other[...]


def meet_kernel(here_ref, near_ref, _0, _1, _2, own_ref, across_ref):
    own_ref[...] = here_ref[0:256, :] + near_ref[0:256, :]
    across_ref[...] = here_ref[256:512, :] + near_ref[256:512, :]


def y_forward_kernel(*refs):
    *parts, table_ref, _, out_ref = refs
    total = parts[0][...]
    for part in parts[1:]:
        total = total + part[0:256, :]
    total = jnp.concatenate([total[0:128], total[128:256]], axis=1)
    out_ref[...] = dot(table_ref[...], stacked(total, 1), ((1,), (1,)))


def pack_kernel(k_ref, send_ref, rows):
    send_ref[...] = jnp.zeros_like(send_ref)
    for k2 in range(2):
        rows[...] = jnp.concatenate([k_ref[0, :, k2].reshape(72, GRID), k_ref[1, :, k2].reshape(72, GRID)], axis=1)
        for i in range(3):
            first = 32 * k2 + 9 * i
            send_ref[first : first + 9, :] = rows[pl.ds(5 + i, 9, stride=8), :]


def spread(value, table):
    high, low = split(value)
    return dot(high, table) + dot(low, table)


def prepare_kernel(k_ref, mirror_ref, coupling_ref, table_ref, k_out, c_out):
    own_table = table_ref[0:80, :]
    other_table = table_ref[80:112, :]
    lanes = table_ref[112:144, :]
    mask = table_ref[144:272, :].astype(F32)
    rest = table_ref[272:400, 0:256].astype(F32)
    flip = rest[0:64, 128:192].astype(BF)
    rows = rest[:, 0:32].astype(BF)
    zeros = jnp.zeros((8, GRID), F32)
    for part in range(2):
        for k2 in range(2):
            place = slice(k2 * 64, k2 * 64 + 64)
            own = jnp.concatenate([k_ref[part, :, k2].reshape(72, GRID), zeros], axis=0).T
            k_out[0, part, place, :] = spread(own, own_table)
            mirror = mirror_ref[32 * k2 : 32 * k2 + 32, 64 * part : 64 * part + 64]
            mirror = spread(mirror, flip).T
            if part == 1:
                mirror = -mirror
            k_out[1, part, place, :] = spread(mirror, other_table)
    high, low = split(spread(coupling_ref[...].T, lanes))
    placed = (dot(rows, high) + dot(rows, low)) * mask
    high, low = split(placed)
    c_out[...] = jnp.concatenate([high, low, high], axis=0)


def middle_kernel(a_ref, forward_ref, c_ref, k_ref, inverse_ref, out_ref):
    value = jnp.concatenate([a_ref[:, sign].reshape(256, 128) for sign in range(2)], axis=1)
    freq = dot(forward_ref[...], stacked(value, 0))
    freq = jnp.concatenate([freq[:, 0:128], freq[:, 128:256]], axis=0)
    terms = dot(stacked(freq, 1), c_ref[...])
    fields = []
    for sign in range(2):
        pieces = []
        for k2 in range(2):
            real = jnp.zeros((64, 128), F32)
            imag = jnp.zeros((64, 128), F32)
            row = sign * 256 + k2 * 128
            for s in range(ORDER + 1):
                lanes = slice(128 * s, 128 * s + 128)
                tr = terms[row : row + 64, lanes]
                ti = terms[row + 64 : row + 128, lanes]
                kr = k_ref[sign, 0, k2 * 64 : k2 * 64 + 64, lanes]
                ki = k_ref[sign, 1, k2 * 64 : k2 * 64 + 64, lanes]
                real = real + kr * tr - ki * ti
                imag = imag + kr * ti + ki * tr
            pieces += [real, imag]
        fields.append(jnp.concatenate(pieces, axis=0))
    result = dot(inverse_ref[...], stacked(jnp.concatenate(fields, axis=1), 0))
    for sign in range(2):
        out_ref[:, sign] = result[:, 128 * sign : 128 * sign + 128].reshape(32, 8, 128)


def y_inverse_kernel(a_ref, table_ref, out_ref):
    result = dot(stacked(a_ref[...].T, 1), table_ref[...])
    out_ref[0:128, :] = result[:, 0:128]
    out_ref[128:256, :] = result[:, 128:256]


def z_inverse_kernel(*refs):
    parts = refs[0:8]
    table_ref, ls, fs = refs[8:]
    row = 0
    for part in parts:
        rows = part.shape[0]
        fs[row : row + rows, :] = part[...]
        row += rows
    me = lax.axis_index("narrow")
    table = table_ref[me]

    def coefficients(g, carry):
        first = g * BATCH
        freqs = []
        for i in range(BATCH):
            rows = []
            for p in range(2):
                for t in range(SLOTS):
                    rows.append(fs[pl.ds(p * 128 + t * NC + first + i, 8, stride=256), :])
            freqs.append(jnp.concatenate(rows, axis=0))
        result = dot(table, stacked(jnp.concatenate(freqs, axis=1), 0))
        for i in range(BATCH):
            plane = result[:, 128 * i : 128 * i + 128].T
            rows = pl.ds(pl.multiple_of((first + i) * 64, 64), 64)
            ls[rows, :] = jnp.concatenate([plane[0:64], plane[64:128]], axis=1)
        return carry

    lax.fori_loop(0, NC // BATCH, coefficients, 0)


def tail_kernel(local_ref, octant_ref, op_ref, out_ref, ws):
    w_cat = load_operators(op_ref, ws)

    def group(g, carry):
        b = g * GROUP
        store_blocks(out_ref, b, *translate(w_cat, load_blocks(local_ref, b), lane_rows(octant_ref, b, GROUP)))
        return carry

    lax.fori_loop(0, 64 // GROUP, group, 0)


def call(kernel, out_shape, scratch=(), in_specs=None):
    args = {}
    if in_specs is not None:
        args["in_specs"] = in_specs
    return pl.pallas_call(
        kernel,
        out_shape=out_shape,
        scratch_shapes=list(scratch),
        compiler_params=pltpu.CompilerParams(vmem_limit_bytes=VMEM_LIMIT),
        **args,
    )


def shape(*dims, dtype=F32):
    return jax.ShapeDtypeStruct(dims, dtype)


Z_FORWARD, Z_INVERSE = z_tables()
Y_FORWARD, Y_INVERSE = y_tables()
X_FORWARD, X_INVERSE = x_tables()
EXPAND = expand_tables()


def block_rows(array):
    lead = array.shape[:-2]
    array = array.reshape(lead + (2, 32, 128))
    array = jnp.swapaxes(array, -3, -2)
    return array.reshape(-1, 128)


def swap(array, partner):
    return lax.ppermute(array, "narrow", [(n, n ^ partner) for n in range(8)])


def shift(array, step):
    return lax.ppermute(array, "narrow", [(n, stepped(n, step, 1)) for n in range(8)])


def shards(leaf_multipoles, leaf_order, subtree_octant, m2m_operators, coupling, kernel_spectrum, l2l_operators):
    leaves = block_rows(leaf_multipoles[0])
    orders = block_rows(leaf_order[0])
    octants = block_rows(subtree_octant[0])
    m2m = jnp.swapaxes(m2m_operators, 0, 1).reshape(NC * 8, NC)
    l2l = jnp.swapaxes(l2l_operators, 0, 1).reshape(NC * 8, NC)
    kernel = kernel_spectrum.transpose(0, 1, 3, 4, 2)

    packed = call(pack_kernel, shape(64, 128), [pltpu.VMEM((72, 128), F32)])(kernel)
    mirror = lax.ppermute(packed, "narrow", [(n, 7 - n) for n in range(8)])
    aux = [(8 * octants + orders).astype(F32), jnp.pad(m2m, ((0, 0), (0, 128 - NC)))]
    moments = call(head_kernel, shape(NC * 64, 128))(leaves, jnp.concatenate(aux, axis=0))
    whole = pl.BlockSpec(memory_space=pltpu.VMEM)
    anywhere = pl.BlockSpec(memory_space=pl.ANY)
    chunks = call(z_forward_kernel, shape(2048, 128))(moments, jnp.asarray(Z_FORWARD))
    chunks = chunks.reshape(8, 256, 128)
    far, mid = call(lift_kernel, (shape(256, 128), shape(256, 128)))(
        chunks[2], chunks[4], swap(chunks[3], 1), swap(chunks[5], 1)
    )
    near = swap(chunks[6:8].reshape(512, 128), 2)
    own, across = call(meet_kernel, (shape(256, 128), shape(256, 128)), (), [whole] * 2 + [anywhere] * 3)(
        chunks[0:2].reshape(512, 128), near, far, mid, mirror
    )
    received = [own, swap(far, 4), swap(mid, 6), swap(across, 1)]

    kernels, couplings = call(prepare_kernel, (shape(2, 2, 128, 640), shape(384, 640, dtype=BF)))(
        kernel, mirror, jnp.pad(coupling, ((0, 32 - NC), (0, 32 - NC))), jnp.asarray(EXPAND)
    )

    along = call(y_forward_kernel, shape(512, 128), (), [whole] * 5 + [anywhere])(*received, jnp.asarray(Y_FORWARD), kernels)
    along = lax.all_to_all(along.reshape(32, 16, 128), "wide", split_axis=0, concat_axis=0, tiled=True)
    along = call(middle_kernel, shape(32, 2, 8, 128))(
        along.reshape(32, 2, 8, 128), jnp.asarray(X_FORWARD), couplings, kernels, jnp.asarray(X_INVERSE)
    )
    along = lax.all_to_all(along.reshape(32, 16, 128), "wide", split_axis=0, concat_axis=0, tiled=True)
    plane = call(y_inverse_kernel, shape(256, 128))(along.reshape(512, 128), jnp.asarray(Y_INVERSE))

    other = shift(plane, ACROSS)
    far = shift(plane, FAR)
    above, below = shift(plane, ABOVE), shift(plane, BELOW)
    far_other, above_other, below_other = shift(far, ACROSS), shift(other, ABOVE), shift(other, BELOW)
    planes = [plane, far, above, below, other, far_other, above_other, below_other]
    local = call(z_inverse_kernel, shape(NC * 64, 128), [pltpu.VMEM((2048, 128), F32)])(*planes, jnp.asarray(Z_INVERSE))
    children = call(tail_kernel, shape(NC * 64, 128), [pltpu.VMEM((256, 128), F32)])(local, octants, l2l)
    children = children.reshape(NC, 32, 2, 128).swapaxes(1, 2)
    return children.reshape(1, NC, 2, 4096)


def solution(mesh):
    return jax.shard_map(
        shards,
        mesh=mesh,
        in_specs=(
            P("narrow", None, "wide", None),
            P("narrow", "wide", None),
            P("narrow", "wide", None),
            P(),
            P(),
            P(None, None, None, "wide", "narrow"),
            P(),
        ),
        out_specs=P("narrow", None, "wide", None),
        check_vma=False,
    )
```

```python
import numpy as np
import ml_dtypes

import jax
import jax.numpy as jnp
from jax import lax
from jax.experimental import pallas as pl
from jax.experimental.pallas import tpu as pltpu
from jax.sharding import PartitionSpec as P

ORDER = 4
GRID = 64
NC = 25
SLOTS = 5
BF = jnp.bfloat16
F32 = jnp.float32
VMEM_LIMIT = 48 * 1024 * 1024

FAR, ABOVE, BELOW, ACROSS = (2, 0), (1, 0), (-1, 0), (0, 1)
GATHER_STEPS = ((0, 0), FAR, ABOVE, BELOW, ACROSS, (2, 1), (1, 1), (-1, 1))
SUM_PARTNERS = (0, 1, 4, 5, 6, 7, 2, 3)

DEGREE = np.array([n for n in range(ORDER + 1) for _ in range(2 * n + 1)])


def halves(table):
    high = table.astype(ml_dtypes.bfloat16)
    low = (table - high.astype(np.float64)).astype(ml_dtypes.bfloat16)
    return high, low


def stack_left(table):
    high, low = halves(table)
    return np.concatenate([high, low, high], axis=1)


def stack_right(table):
    high, low = halves(table)
    return np.concatenate([high, low, high], axis=0)


def wave(a, b):
    angle = 2.0 * np.pi * ((a * b) % GRID) / GRID
    return np.cos(angle), np.sin(angle)


def complex_table(cosine, sine, sign):
    return np.stack([np.stack([cosine, -sign * sine]), np.stack([sign * sine, cosine])])


def stepped(n, step, sign):
    return (n // 2 + sign * step[0]) % 4 * 2 + (n + step[1]) % 2


def z_tables():
    z = np.arange(GRID)
    forward, inverse = [], []
    for n in range(8):
        tables = []
        towards = [n ^ partner for partner in SUM_PARTNERS]
        origins = [stepped(n, step, -1) for step in GATHER_STEPS]
        for devices in (towards, origins):
            rows = [8 * device + t for t in range(SLOTS) for device in devices]
            cosine, sine = wave(np.array(rows)[:, None], z[None, :])
            tables.append(np.concatenate([cosine, -sine], axis=0))
        forward.append(stack_left(tables[0]))
        inverse.append(stack_left(tables[1].T / GRID))
    return np.stack(forward), np.stack(inverse)


def y_tables():
    ky = np.arange(GRID)

    def place(table):
        table = table.reshape(2, 2, 2, 32, 2, 32, 2)
        table = table.transpose(3, 0, 4, 1, 2, 6, 5)
        full = np.zeros((32, 2, 2, 2, 2, 2, 2, 32, 2))
        for xl in range(2):
            full[:, :, xl, :, :, :, :, :, xl] = table
        return full

    waves = [wave(sign * ky[:, None], ky[None, :]) for sign in (1, -1)]
    forward = np.stack([complex_table(*w, -1) for w in waves])
    back = np.stack([complex_table(*w, 1).transpose(1, 0, 2, 3) for w in waves]) / GRID
    forward = place(forward).reshape(512, 256)
    inverse = place(back).reshape(512, 256)
    return stack_left(forward), stack_right(inverse)


def x_tables():
    kx = np.arange(GRID)
    cosine, sine = wave(kx[:, None], kx[None, :])

    def place(table):
        table = table.reshape(2, 2, GRID, 32, 2).transpose(0, 2, 3, 4, 1)
        full = np.zeros((2, 2, GRID, 32, 2, 2, 2))
        for k2 in range(2):
            full[k2, :, :, :, :, k2, :] = table
        return full.reshape(256, 256)

    forward = place(complex_table(cosine, sine, -1))
    back = complex_table(cosine, sine, 1) / GRID
    inverse = place(back.transpose(1, 0, 2, 3)).T
    return stack_left(forward), stack_left(inverse)


def expand_tables():
    own = np.zeros((72, 640), np.float32)
    mirror = np.zeros((32, 640), np.float32)
    rows = np.zeros((128, NC), np.float32)
    lanes = np.zeros((NC, 640), np.float32)
    mask = np.zeros((128, 640), np.float32)
    for t in range(SLOTS):
        for c in range(NC):
            rows[t * NC + c, c] = 1
            for s in range(ORDER + 1):
                lane = s * 128 + t * NC + c
                lanes[c, lane] = 1
                d = DEGREE[c] + s
                own[d * 8 + t, lane] = 1
                if 1 <= t <= 3:
                    mirror[(3 - t) * 9 + d, lane] = 1
                for j in range(NC):
                    if DEGREE[j] == s:
                        mask[t * NC + j, lane] = 1
    flip = np.zeros((GRID, GRID), np.float32)
    for k in range(GRID):
        flip[(-k) % GRID, k] = 1
    table = np.zeros((400, 640), ml_dtypes.bfloat16)
    table[0:72], table[80:112], table[112:137], table[144:272] = own, mirror, lanes, mask
    table[272:400, 0:NC], table[272:336, 128:192] = rows, flip
    return table


def split(value):
    high = value.astype(BF)
    low = (value - high.astype(F32)).astype(BF)
    return high, low


def stacked(value, axis):
    high, low = split(value)
    return jnp.concatenate([high, high, low], axis=axis)


def dot(a, b, dims=((1,), (0,)), precision=None):
    return lax.dot_general(a, b, (dims, ((), ())), precision=precision, preferred_element_type=F32)


def degree_column():
    row = lax.broadcasted_iota(jnp.int32, (32, 1), 0)
    one = lambda bound: (row >= bound).astype(jnp.int32)
    return one(1) + one(4) + one(9) + one(16) + 90 * one(25)


def load_operators(op_ref, w_ref):
    w_ref[...] = jnp.zeros_like(w_ref)
    w_ref[0:200, 0:NC] = op_ref[...]
    return operator_rows(w_ref, 0)


def operator_rows(ref, first):
    rows = [ref[pl.ds(first + octant, 24, stride=8), :] for octant in range(8)] + [ref[first + 192 : first + 200, :]]
    high, low = split(jnp.concatenate(rows, axis=0)[:, 0:32])
    return jnp.concatenate([high, low, high], axis=1)


def load_blocks(ref, first):
    blocks = []
    for i in range(GROUP):
        last = ref[pl.ds(24 * 64 + first + i, 1), :]
        blocks.append(jnp.concatenate([ref[pl.ds(first + i, 24, stride=64), :], jnp.broadcast_to(last, (8, 128))], axis=0))
    return jnp.concatenate(blocks, axis=1)


def store_blocks(ref, first, most, last):
    for i in range(GROUP):
        lanes = slice(128 * i, 128 * i + 128)
        ref[pl.ds(first + i, 24, stride=64), :] = most[:, lanes]
        ref[pl.ds(24 * 64 + first + i, 1), :] = last[:, lanes]


def lane_rows(ref, first, count):
    return jnp.concatenate([ref[pl.ds(first + i, 1), :] for i in range(count)], axis=1)


def translate(w_cat, value, octant):
    product = dot(w_cat, stacked(value, 0))
    total = product[0:24]
    for o in range(1, 8):
        total = jnp.where(octant == o, product[24 * o : 24 * o + 24], total)
    chosen = octant == lax.broadcasted_iota(jnp.int32, (8, 1), 0)
    last = jnp.sum(jnp.where(chosen, product[192:200], 0.0), axis=0, keepdims=True)
    return total, last


GROUP = 64
BATCH = 25


def head_kernel(leaf_hbm, order_hbm, octant_hbm, op_hbm, out_ref, leaf_ref, order_ref, octant_ref, op_ref, ws, sems):
    ends = [(op_hbm, op_ref), (order_hbm, order_ref), (octant_hbm, octant_ref), (leaf_hbm, leaf_ref)]
    copies = [pltpu.make_async_copy(a, b, sems.at[i]) for i, (a, b) in enumerate(ends)]
    for copy in copies:
        copy.start()
    copies[0].wait()
    w_cat = load_operators(op_ref, ws)
    degree = degree_column()
    for copy in copies[1:]:
        copy.wait()

    def group(g, carry):
        b = g * GROUP
        kept = jnp.where(degree <= lane_rows(order_ref, b, GROUP), load_blocks(leaf_ref, b), 0.0)
        store_blocks(out_ref, b, *translate(w_cat, kept, lane_rows(octant_ref, b, GROUP)))
        return carry

    lax.fori_loop(0, 64 // GROUP, group, 0)


def z_forward_kernel(ms, table_ref, out_ref):
    me = lax.axis_index("narrow")
    table = table_ref[me]
    for m in range(16):
        out_ref[m * 128 + 120 : m * 128 + 128, :] = jnp.zeros((8, 128), F32)

    def coefficients(g, carry):
        first = g * BATCH
        rows = pl.ds(pl.multiple_of(first * 64, 64), 64 * BATCH)
        pieces = []
        for part in split(ms[rows, :]):
            halves_ = [part[64 * i : 64 * i + 64, 64 * y2 : 64 * y2 + 64] for i in range(BATCH) for y2 in range(2)]
            pieces.append(jnp.concatenate(halves_, axis=0))
        high, low = pieces
        result = dot(table, jnp.concatenate([high, high, low], axis=1), ((1,), (1,)))
        for i in range(BATCH):
            for p in range(2):
                for t in range(SLOTS):
                    row = 40 * p + 8 * t
                    value = result[row : row + 8, 128 * i : 128 * i + 128]
                    out_ref[pl.ds(p * 128 + t * NC + first + i, 8, stride=256), :] = value
        return carry

    lax.fori_loop(0, NC // BATCH, coefficients, 0)


def lift_kernel(far_ref, mid_ref, far_other, mid_other, far_out, mid_out):
    far_out[...] = far_ref[...] + far_other[...]
    mid_out[...] = mid_ref[...] + mid_other[...]


def meet_kernel(here_ref, near_ref, _0, _1, _2, own_ref, across_ref):
    own_ref[...] = here_ref[0:256, :] + near_ref[0:256, :]
    across_ref[...] = here_ref[256:512, :] + near_ref[256:512, :]


def y_forward_kernel(*refs):
    *parts, table_ref, _, out_ref = refs
    total = parts[0][...]
    for part in parts[1:]:
        total = total + part[0:256, :]
    total = jnp.concatenate([total[0:128], total[128:256]], axis=1)
    out_ref[...] = dot(table_ref[...], stacked(total, 1), ((1,), (1,)))


def pack_kernel(k_ref, send_ref, rows):
    send_ref[...] = jnp.zeros_like(send_ref)
    for k2 in range(2):
        rows[...] = jnp.concatenate([k_ref[0, :, k2].reshape(72, GRID), k_ref[1, :, k2].reshape(72, GRID)], axis=1)
        for i in range(3):
            first = 32 * k2 + 9 * i
            send_ref[first : first + 9, :] = rows[pl.ds(5 + i, 9, stride=8), :]


def spread(value, table):
    high, low = split(value)
    return dot(high, table) + dot(low, table)


def prepare_kernel(k_ref, mirror_ref, coupling_ref, table_ref, k_out, c_out):
    own_table = table_ref[0:80, :]
    other_table = table_ref[80:112, :]
    lanes = table_ref[112:144, :]
    mask = table_ref[144:272, :].astype(F32)
    rest = table_ref[272:400, 0:256].astype(F32)
    flip = rest[0:64, 128:192].astype(BF)
    rows = rest[:, 0:32].astype(BF)
    zeros = jnp.zeros((8, GRID), F32)
    for part in range(2):
        for k2 in range(2):
            place = slice(k2 * 64, k2 * 64 + 64)
            own = jnp.concatenate([k_ref[part, :, k2].reshape(72, GRID), zeros], axis=0).T
            k_out[0, part, place, :] = spread(own, own_table)
            mirror = mirror_ref[32 * k2 : 32 * k2 + 32, 64 * part : 64 * part + 64]
            mirror = spread(mirror, flip).T
            if part == 1:
                mirror = -mirror
            k_out[1, part, place, :] = spread(mirror, other_table)
    high, low = split(spread(coupling_ref[...].T, lanes))
    placed = (dot(rows, high) + dot(rows, low)) * mask
    high, low = split(placed)
    c_out[...] = jnp.concatenate([high, low, high], axis=0)


def middle_kernel(a_ref, forward_ref, c_ref, k_ref, inverse_ref, out_ref):
    value = jnp.concatenate([a_ref[:, sign].reshape(256, 128) for sign in range(2)], axis=1)
    freq = dot(forward_ref[...], stacked(value, 0))
    freq = jnp.concatenate([freq[:, 0:128], freq[:, 128:256]], axis=0)
    terms = dot(stacked(freq, 1), c_ref[...])
    fields = []
    for sign in range(2):
        pieces = []
        for k2 in range(2):
            real = jnp.zeros((64, 128), F32)
            imag = jnp.zeros((64, 128), F32)
            row = sign * 256 + k2 * 128
            for s in range(ORDER + 1):
                lanes = slice(128 * s, 128 * s + 128)
                tr = terms[row : row + 64, lanes]
                ti = terms[row + 64 : row + 128, lanes]
                kr = k_ref[sign, 0, k2 * 64 : k2 * 64 + 64, lanes]
                ki = k_ref[sign, 1, k2 * 64 : k2 * 64 + 64, lanes]
                real = real + kr * tr - ki * ti
                imag = imag + kr * ti + ki * tr
            pieces += [real, imag]
        fields.append(jnp.concatenate(pieces, axis=0))
    result = dot(inverse_ref[...], stacked(jnp.concatenate(fields, axis=1), 0))
    for sign in range(2):
        out_ref[:, sign] = result[:, 128 * sign : 128 * sign + 128].reshape(32, 8, 128)


def y_inverse_kernel(a_ref, table_ref, out_ref):
    result = dot(stacked(a_ref[...].T, 1), table_ref[...])
    out_ref[0:128, :] = result[:, 0:128]
    out_ref[128:256, :] = result[:, 128:256]


def z_inverse_kernel(*refs):
    parts = refs[0:8]
    table_ref, ls, fs = refs[8:]
    row = 0
    for part in parts:
        rows = part.shape[0]
        fs[row : row + rows, :] = part[...]
        row += rows
    me = lax.axis_index("narrow")
    table = table_ref[me]

    def coefficients(g, carry):
        first = g * BATCH
        freqs = []
        for i in range(BATCH):
            rows = []
            for p in range(2):
                for t in range(SLOTS):
                    rows.append(fs[pl.ds(p * 128 + t * NC + first + i, 8, stride=256), :])
            freqs.append(jnp.concatenate(rows, axis=0))
        result = dot(table, stacked(jnp.concatenate(freqs, axis=1), 0))
        for i in range(BATCH):
            plane = result[:, 128 * i : 128 * i + 128].T
            rows = pl.ds(pl.multiple_of((first + i) * 64, 64), 64)
            ls[rows, :] = jnp.concatenate([plane[0:64], plane[64:128]], axis=1)
        return carry

    lax.fori_loop(0, NC // BATCH, coefficients, 0)


def tail_kernel(local_ref, octant_ref, op_ref, out_ref, ws):
    w_cat = load_operators(op_ref, ws)

    def group(g, carry):
        b = g * GROUP
        store_blocks(out_ref, b, *translate(w_cat, load_blocks(local_ref, b), lane_rows(octant_ref, b, GROUP)))
        return carry

    lax.fori_loop(0, 64 // GROUP, group, 0)


def call(kernel, out_shape, scratch=(), in_specs=None):
    args = {}
    if in_specs is not None:
        args["in_specs"] = in_specs
    return pl.pallas_call(
        kernel,
        out_shape=out_shape,
        scratch_shapes=list(scratch),
        compiler_params=pltpu.CompilerParams(vmem_limit_bytes=VMEM_LIMIT),
        **args,
    )


def shape(*dims, dtype=F32):
    return jax.ShapeDtypeStruct(dims, dtype)


Z_FORWARD, Z_INVERSE = z_tables()
Y_FORWARD, Y_INVERSE = y_tables()
X_FORWARD, X_INVERSE = x_tables()
EXPAND = expand_tables()


def block_rows(array):
    lead = array.shape[:-2]
    array = array.reshape(lead + (2, 32, 128))
    array = jnp.swapaxes(array, -3, -2)
    return array.reshape(-1, 128)


def swap(array, partner):
    return lax.ppermute(array, "narrow", [(n, n ^ partner) for n in range(8)])


def shift(array, step):
    return lax.ppermute(array, "narrow", [(n, stepped(n, step, 1)) for n in range(8)])


def shards(leaf_multipoles, leaf_order, subtree_octant, m2m_operators, coupling, kernel_spectrum, l2l_operators):
    leaves = block_rows(leaf_multipoles[0])
    orders = block_rows(leaf_order[0])
    octants = block_rows(subtree_octant[0])
    m2m = jnp.swapaxes(m2m_operators, 0, 1).reshape(NC * 8, NC)
    l2l = jnp.swapaxes(l2l_operators, 0, 1).reshape(NC * 8, NC)
    kernel = kernel_spectrum.transpose(0, 1, 3, 4, 2)

    packed = call(pack_kernel, shape(64, 128), [pltpu.VMEM((72, 128), F32)])(kernel)
    mirror = lax.ppermute(packed, "narrow", [(n, 7 - n) for n in range(8)])
    inputs = [pltpu.with_memory_space_constraint(array, pltpu.HBM) for array in (leaves, orders, octants, m2m)]
    moments = call(
        head_kernel,
        shape(NC * 64, 128),
        [
            pltpu.VMEM((NC * 64, 128), F32),
            pltpu.VMEM((64, 128), jnp.int32),
            pltpu.VMEM((64, 128), jnp.int32),
            pltpu.VMEM((NC * 8, NC), F32),
            pltpu.VMEM((256, 128), F32),
            pltpu.SemaphoreType.DMA((4,)),
        ],
        [pl.BlockSpec(memory_space=pltpu.HBM)] * 4,
    )(*inputs)
    whole = pl.BlockSpec(memory_space=pltpu.VMEM)
    anywhere = pl.BlockSpec(memory_space=pl.ANY)
    chunks = call(z_forward_kernel, shape(2048, 128))(moments, jnp.asarray(Z_FORWARD))
    chunks = chunks.reshape(8, 256, 128)
    far, mid = call(lift_kernel, (shape(256, 128), shape(256, 128)))(
        chunks[2], chunks[4], swap(chunks[3], 1), swap(chunks[5], 1)
    )
    near = swap(chunks[6:8].reshape(512, 128), 2)
    own, across = call(meet_kernel, (shape(256, 128), shape(256, 128)), (), [whole] * 2 + [anywhere] * 3)(
        chunks[0:2].reshape(512, 128), near, far, mid, mirror
    )
    received = [own, swap(far, 4), swap(mid, 6), swap(across, 1)]

    kernels, couplings = call(prepare_kernel, (shape(2, 2, 128, 640), shape(384, 640, dtype=BF)))(
        kernel, mirror, jnp.pad(coupling, ((0, 32 - NC), (0, 32 - NC))), jnp.asarray(EXPAND)
    )

    along = call(y_forward_kernel, shape(512, 128), (), [whole] * 5 + [anywhere])(*received, jnp.asarray(Y_FORWARD), kernels)
    along = lax.all_to_all(along.reshape(32, 16, 128), "wide", split_axis=0, concat_axis=0, tiled=True)
    along = call(middle_kernel, shape(32, 2, 8, 128))(
        along.reshape(32, 2, 8, 128), jnp.asarray(X_FORWARD), couplings, kernels, jnp.asarray(X_INVERSE)
    )
    along = lax.all_to_all(along.reshape(32, 16, 128), "wide", split_axis=0, concat_axis=0, tiled=True)
    plane = call(y_inverse_kernel, shape(256, 128))(along.reshape(512, 128), jnp.asarray(Y_INVERSE))

    other = shift(plane, ACROSS)
    far = shift(plane, FAR)
    above, below = shift(plane, ABOVE), shift(plane, BELOW)
    far_other, above_other, below_other = shift(far, ACROSS), shift(other, ABOVE), shift(other, BELOW)
    planes = [plane, far, above, below, other, far_other, above_other, below_other]
    local = call(z_inverse_kernel, shape(NC * 64, 128), [pltpu.VMEM((2048, 128), F32)])(*planes, jnp.asarray(Z_INVERSE))
    children = call(tail_kernel, shape(NC * 64, 128), [pltpu.VMEM((256, 128), F32)])(local, octants, l2l)
    children = children.reshape(NC, 32, 2, 128).swapaxes(1, 2)
    return children.reshape(1, NC, 2, 4096)


def solution(mesh):
    return jax.shard_map(
        shards,
        mesh=mesh,
        in_specs=(
            P("narrow", None, "wide", None),
            P("narrow", "wide", None),
            P("narrow", "wide", None),
            P(),
            P(),
            P(None, None, None, "wide", "narrow"),
            P(),
        ),
        out_specs=P("narrow", None, "wide", None),
        check_vma=False,
    )
```

```python
import numpy as np
import ml_dtypes

import jax
import jax.numpy as jnp
from jax import lax
from jax.experimental import pallas as pl
from jax.experimental.pallas import tpu as pltpu
from jax.sharding import PartitionSpec as P

ORDER = 4
GRID = 64
NC = 25
SLOTS = 5
BF = jnp.bfloat16
F32 = jnp.float32
VMEM_LIMIT = 48 * 1024 * 1024

FAR, ABOVE, BELOW, ACROSS = (2, 0), (1, 0), (-1, 0), (0, 1)
GATHER_STEPS = ((0, 0), FAR, ABOVE, BELOW, ACROSS, (2, 1), (1, 1), (-1, 1))
SUM_PARTNERS = (0, 1, 4, 5, 6, 7, 2, 3)

DEGREE = np.array([n for n in range(ORDER + 1) for _ in range(2 * n + 1)])


def halves(table):
    high = table.astype(ml_dtypes.bfloat16)
    low = (table - high.astype(np.float64)).astype(ml_dtypes.bfloat16)
    return high, low


def stack_left(table):
    high, low = halves(table)
    return np.concatenate([high, low, high], axis=1)


def stack_right(table):
    high, low = halves(table)
    return np.concatenate([high, low, high], axis=0)


def wave(a, b):
    angle = 2.0 * np.pi * ((a * b) % GRID) / GRID
    return np.cos(angle), np.sin(angle)


def complex_table(cosine, sine, sign):
    return np.stack([np.stack([cosine, -sign * sine]), np.stack([sign * sine, cosine])])


def stepped(n, step, sign):
    return (n // 2 + sign * step[0]) % 4 * 2 + (n + step[1]) % 2


def z_tables():
    z = np.arange(GRID)
    forward, inverse = [], []
    for n in range(8):
        tables = []
        towards = [n ^ partner for partner in SUM_PARTNERS]
        origins = [stepped(n, step, -1) for step in GATHER_STEPS]
        for devices in (towards, origins):
            rows = [8 * device + t for t in range(SLOTS) for device in devices]
            cosine, sine = wave(np.array(rows)[:, None], z[None, :])
            tables.append(np.concatenate([cosine, -sine], axis=0))
        forward.append(stack_left(tables[0]))
        inverse.append(stack_left(tables[1].T / GRID))
    return np.stack(forward), np.stack(inverse)


def y_tables():
    ky = np.arange(GRID)

    def place(table):
        table = table.reshape(2, 2, 2, 32, 2, 32, 2)
        table = table.transpose(3, 0, 4, 1, 2, 6, 5)
        full = np.zeros((32, 2, 2, 2, 2, 2, 2, 32, 2))
        for xl in range(2):
            full[:, :, xl, :, :, :, :, :, xl] = table
        return full

    waves = [wave(sign * ky[:, None], ky[None, :]) for sign in (1, -1)]
    forward = np.stack([complex_table(*w, -1) for w in waves])
    back = np.stack([complex_table(*w, 1).transpose(1, 0, 2, 3) for w in waves]) / GRID
    forward = place(forward).reshape(512, 256)
    inverse = place(back).reshape(512, 256)
    return stack_left(forward), stack_right(inverse)


def x_tables():
    kx = np.arange(GRID)
    cosine, sine = wave(kx[:, None], kx[None, :])

    def place(table):
        table = table.reshape(2, 2, GRID, 32, 2).transpose(0, 2, 3, 4, 1)
        full = np.zeros((2, 2, GRID, 32, 2, 2, 2))
        for k2 in range(2):
            full[k2, :, :, :, :, k2, :] = table
        return full.reshape(256, 256)

    forward = place(complex_table(cosine, sine, -1))
    back = complex_table(cosine, sine, 1) / GRID
    inverse = place(back.transpose(1, 0, 2, 3)).T
    return stack_left(forward), stack_left(inverse)


def expand_tables():
    own = np.zeros((72, 640), np.float32)
    mirror = np.zeros((32, 640), np.float32)
    rows = np.zeros((128, NC), np.float32)
    lanes = np.zeros((NC, 640), np.float32)
    mask = np.zeros((128, 640), np.float32)
    for t in range(SLOTS):
        for c in range(NC):
            rows[t * NC + c, c] = 1
            for s in range(ORDER + 1):
                lane = s * 128 + t * NC + c
                lanes[c, lane] = 1
                d = DEGREE[c] + s
                own[d * 8 + t, lane] = 1
                if 1 <= t <= 3:
                    mirror[(3 - t) * 9 + d, lane] = 1
                for j in range(NC):
                    if DEGREE[j] == s:
                        mask[t * NC + j, lane] = 1
    flip = np.zeros((GRID, GRID), np.float32)
    for k in range(GRID):
        flip[(-k) % GRID, k] = 1
    table = np.zeros((400, 640), ml_dtypes.bfloat16)
    table[0:72], table[80:112], table[112:137], table[144:272] = own, mirror, lanes, mask
    table[272:400, 0:NC], table[272:336, 128:192] = rows, flip
    return table


def split(value):
    high = value.astype(BF)
    low = (value - high.astype(F32)).astype(BF)
    return high, low


def stacked(value, axis):
    high, low = split(value)
    return jnp.concatenate([high, high, low], axis=axis)


def dot(a, b, dims=((1,), (0,)), precision=None):
    return lax.dot_general(a, b, (dims, ((), ())), precision=precision, preferred_element_type=F32)


def degree_column():
    row = lax.broadcasted_iota(jnp.int32, (32, 1), 0)
    one = lambda bound: (row >= bound).astype(jnp.int32)
    return one(1) + one(4) + one(9) + one(16) + 90 * one(25)


def load_operators(op_ref, w_ref):
    w_ref[...] = jnp.zeros_like(w_ref)
    w_ref[0:200, 0:NC] = op_ref[...]
    return operator_rows(w_ref, 0)


def operator_rows(ref, first):
    rows = [ref[pl.ds(first + octant, 24, stride=8), :] for octant in range(8)] + [ref[first + 192 : first + 200, :]]
    high, low = split(jnp.concatenate(rows, axis=0)[:, 0:32])
    return jnp.concatenate([high, low, high], axis=1)


def load_blocks(ref, first):
    blocks = []
    for i in range(GROUP):
        last = ref[pl.ds(24 * 64 + first + i, 1), :]
        blocks.append(jnp.concatenate([ref[pl.ds(first + i, 24, stride=64), :], jnp.broadcast_to(last, (8, 128))], axis=0))
    return jnp.concatenate(blocks, axis=1)


def store_blocks(ref, first, most, last):
    for i in range(GROUP):
        lanes = slice(128 * i, 128 * i + 128)
        ref[pl.ds(first + i, 24, stride=64), :] = most[:, lanes]
        ref[pl.ds(24 * 64 + first + i, 1), :] = last[:, lanes]


def lane_rows(ref, first, count):
    return jnp.concatenate([ref[pl.ds(first + i, 1), :] for i in range(count)], axis=1)


def translate(w_cat, value, octant):
    product = dot(w_cat, stacked(value, 0))
    total = product[0:24]
    for o in range(1, 8):
        total = jnp.where(octant == o, product[24 * o : 24 * o + 24], total)
    chosen = octant == lax.broadcasted_iota(jnp.int32, (8, 1), 0)
    last = jnp.sum(jnp.where(chosen, product[192:200], 0.0), axis=0, keepdims=True)
    return total, last


GROUP = 32
BATCH = 25


def head_kernel(leaf_hbm, order_hbm, octant_hbm, op_hbm, out_ref, leaf_ref, order_ref, octant_ref, op_ref, ws, sems):
    ends = [(op_hbm, op_ref), (order_hbm, order_ref), (octant_hbm, octant_ref), (leaf_hbm, leaf_ref)]
    copies = [pltpu.make_async_copy(a, b, sems.at[i]) for i, (a, b) in enumerate(ends)]
    for copy in copies:
        copy.start()
    copies[0].wait()
    w_cat = load_operators(op_ref, ws)
    degree = degree_column()
    for copy in copies[1:]:
        copy.wait()

    def group(g, carry):
        b = g * GROUP
        kept = jnp.where(degree <= lane_rows(order_ref, b, GROUP), load_blocks(leaf_ref, b), 0.0)
        store_blocks(out_ref, b, *translate(w_cat, kept, lane_rows(octant_ref, b, GROUP)))
        return carry

    lax.fori_loop(0, 64 // GROUP, group, 0)


def z_forward_kernel(ms, table_ref, out_ref):
    me = lax.axis_index("narrow")
    table = table_ref[me]
    for m in range(16):
        out_ref[m * 128 + 120 : m * 128 + 128, :] = jnp.zeros((8, 128), F32)

    def coefficients(g, carry):
        first = g * BATCH
        rows = pl.ds(pl.multiple_of(first * 64, 64), 64 * BATCH)
        pieces = []
        for part in split(ms[rows, :]):
            halves_ = [part[64 * i : 64 * i + 64, 64 * y2 : 64 * y2 + 64] for i in range(BATCH) for y2 in range(2)]
            pieces.append(jnp.concatenate(halves_, axis=0))
        high, low = pieces
        result = dot(table, jnp.concatenate([high, high, low], axis=1), ((1,), (1,)))
        for i in range(BATCH):
            for p in range(2):
                for t in range(SLOTS):
                    row = 40 * p + 8 * t
                    value = result[row : row + 8, 128 * i : 128 * i + 128]
                    out_ref[pl.ds(p * 128 + t * NC + first + i, 8, stride=256), :] = value
        return carry

    lax.fori_loop(0, NC // BATCH, coefficients, 0)


def lift_kernel(far_ref, mid_ref, far_other, mid_other, far_out, mid_out):
    far_out[...] = far_ref[...] + far_other[...]
    mid_out[...] = mid_ref[...] + mid_other[...]


def meet_kernel(here_ref, near_ref, _0, _1, _2, own_ref, across_ref):
    own_ref[...] = here_ref[0:256, :] + near_ref[0:256, :]
    across_ref[...] = here_ref[256:512, :] + near_ref[256:512, :]


def y_forward_kernel(*refs):
    *parts, table_ref, _, out_ref = refs
    total = parts[0][...]
    for part in parts[1:]:
        total = total + part[0:256, :]
    total = jnp.concatenate([total[0:128], total[128:256]], axis=1)
    out_ref[...] = dot(table_ref[...], stacked(total, 1), ((1,), (1,)))


def pack_kernel(k_ref, send_ref, rows):
    send_ref[...] = jnp.zeros_like(send_ref)
    for k2 in range(2):
        rows[...] = jnp.concatenate([k_ref[0, :, k2].reshape(72, GRID), k_ref[1, :, k2].reshape(72, GRID)], axis=1)
        for i in range(3):
            first = 32 * k2 + 9 * i
            send_ref[first : first + 9, :] = rows[pl.ds(5 + i, 9, stride=8), :]


def spread(value, table):
    high, low = split(value)
    return dot(high, table) + dot(low, table)


def prepare_kernel(k_ref, mirror_ref, coupling_ref, table_ref, k_out, c_out):
    own_table = table_ref[0:80, :]
    other_table = table_ref[80:112, :]
    lanes = table_ref[112:144, :]
    mask = table_ref[144:272, :].astype(F32)
    rest = table_ref[272:400, 0:256].astype(F32)
    flip = rest[0:64, 128:192].astype(BF)
    rows = rest[:, 0:32].astype(BF)
    zeros = jnp.zeros((8, GRID), F32)
    for part in range(2):
        for k2 in range(2):
            place = slice(k2 * 64, k2 * 64 + 64)
            own = jnp.concatenate([k_ref[part, :, k2].reshape(72, GRID), zeros], axis=0).T
            k_out[0, part, place, :] = spread(own, own_table)
            mirror = mirror_ref[32 * k2 : 32 * k2 + 32, 64 * part : 64 * part + 64]
            mirror = spread(mirror, flip).T
            if part == 1:
                mirror = -mirror
            k_out[1, part, place, :] = spread(mirror, other_table)
    high, low = split(spread(coupling_ref[...].T, lanes))
    placed = (dot(rows, high) + dot(rows, low)) * mask
    high, low = split(placed)
    c_out[...] = jnp.concatenate([high, low, high], axis=0)


def middle_kernel(a_ref, forward_ref, c_ref, k_ref, inverse_ref, out_ref):
    value = jnp.concatenate([a_ref[:, sign].reshape(256, 128) for sign in range(2)], axis=1)
    freq = dot(forward_ref[...], stacked(value, 0))
    freq = jnp.concatenate([freq[:, 0:128], freq[:, 128:256]], axis=0)
    terms = dot(stacked(freq, 1), c_ref[...])
    fields = []
    for sign in range(2):
        pieces = []
        for k2 in range(2):
            real = jnp.zeros((64, 128), F32)
            imag = jnp.zeros((64, 128), F32)
            row = sign * 256 + k2 * 128
            for s in range(ORDER + 1):
                lanes = slice(128 * s, 128 * s + 128)
                tr = terms[row : row + 64, lanes]
                ti = terms[row + 64 : row + 128, lanes]
                kr = k_ref[sign, 0, k2 * 64 : k2 * 64 + 64, lanes]
                ki = k_ref[sign, 1, k2 * 64 : k2 * 64 + 64, lanes]
                real = real + kr * tr - ki * ti
                imag = imag + kr * ti + ki * tr
            pieces += [real, imag]
        fields.append(jnp.concatenate(pieces, axis=0))
    result = dot(inverse_ref[...], stacked(jnp.concatenate(fields, axis=1), 0))
    for sign in range(2):
        out_ref[:, sign] = result[:, 128 * sign : 128 * sign + 128].reshape(32, 8, 128)


def y_inverse_kernel(a_ref, table_ref, out_ref):
    result = dot(stacked(a_ref[...].T, 1), table_ref[...])
    out_ref[0:128, :] = result[:, 0:128]
    out_ref[128:256, :] = result[:, 128:256]


def z_inverse_kernel(*refs):
    parts = refs[0:8]
    table_ref, ls, fs = refs[8:]
    row = 0
    for part in parts:
        rows = part.shape[0]
        fs[row : row + rows, :] = part[...]
        row += rows
    me = lax.axis_index("narrow")
    table = table_ref[me]

    def coefficients(g, carry):
        first = g * BATCH
        freqs = []
        for i in range(BATCH):
            rows = []
            for p in range(2):
                for t in range(SLOTS):
                    rows.append(fs[pl.ds(p * 128 + t * NC + first + i, 8, stride=256), :])
            freqs.append(jnp.concatenate(rows, axis=0))
        result = dot(table, stacked(jnp.concatenate(freqs, axis=1), 0))
        for i in range(BATCH):
            plane = result[:, 128 * i : 128 * i + 128].T
            rows = pl.ds(pl.multiple_of((first + i) * 64, 64), 64)
            ls[rows, :] = jnp.concatenate([plane[0:64], plane[64:128]], axis=1)
        return carry

    lax.fori_loop(0, NC // BATCH, coefficients, 0)


def tail_kernel(local_ref, octant_ref, op_ref, out_hbm, ws, out_ref, sems):
    w_cat = load_operators(op_ref, ws)
    copies = []
    for half in range(2):
        for b in range(32 * half, 32 * half + 32, GROUP):
            store_blocks(out_ref, b, *translate(w_cat, load_blocks(local_ref, b), lane_rows(octant_ref, b, GROUP)))
        rows = pl.ds(32 * half, 32)
        done = out_ref.reshape(NC, 64, 128).at[:, rows]
        copies.append(pltpu.make_async_copy(done, out_hbm.at[:, rows], sems.at[half]))
        copies[half].start()
    for copy in copies:
        copy.wait()


def call(kernel, out_shape, scratch=(), in_specs=None, out_specs=None):
    args = {}
    if out_specs is not None:
        args["out_specs"] = out_specs
    if in_specs is not None:
        args["in_specs"] = in_specs
    return pl.pallas_call(
        kernel,
        out_shape=out_shape,
        scratch_shapes=list(scratch),
        compiler_params=pltpu.CompilerParams(vmem_limit_bytes=VMEM_LIMIT),
        **args,
    )


def shape(*dims, dtype=F32):
    return jax.ShapeDtypeStruct(dims, dtype)


Z_FORWARD, Z_INVERSE = z_tables()
Y_FORWARD, Y_INVERSE = y_tables()
X_FORWARD, X_INVERSE = x_tables()
EXPAND = expand_tables()


def block_rows(array):
    lead = array.shape[:-2]
    array = array.reshape(lead + (2, 32, 128))
    array = jnp.swapaxes(array, -3, -2)
    return array.reshape(-1, 128)


def swap(array, partner):
    return lax.ppermute(array, "narrow", [(n, n ^ partner) for n in range(8)])


def shift(array, step):
    return lax.ppermute(array, "narrow", [(n, stepped(n, step, 1)) for n in range(8)])


def shards(leaf_multipoles, leaf_order, subtree_octant, m2m_operators, coupling, kernel_spectrum, l2l_operators):
    leaves = block_rows(leaf_multipoles[0])
    orders = block_rows(leaf_order[0])
    octants = block_rows(subtree_octant[0])
    m2m = jnp.swapaxes(m2m_operators, 0, 1).reshape(NC * 8, NC)
    l2l = jnp.swapaxes(l2l_operators, 0, 1).reshape(NC * 8, NC)
    kernel = kernel_spectrum.transpose(0, 1, 3, 4, 2)

    packed = call(pack_kernel, shape(64, 128), [pltpu.VMEM((72, 128), F32)])(kernel)
    mirror = lax.ppermute(packed, "narrow", [(n, 7 - n) for n in range(8)])
    inputs = [pltpu.with_memory_space_constraint(array, pltpu.HBM) for array in (leaves, orders, octants, m2m)]
    moments = call(
        head_kernel,
        shape(NC * 64, 128),
        [
            pltpu.VMEM((NC * 64, 128), F32),
            pltpu.VMEM((64, 128), jnp.int32),
            pltpu.VMEM((64, 128), jnp.int32),
            pltpu.VMEM((NC * 8, NC), F32),
            pltpu.VMEM((256, 128), F32),
            pltpu.SemaphoreType.DMA((4,)),
        ],
        [pl.BlockSpec(memory_space=pltpu.HBM)] * 4,
    )(*inputs)
    whole = pl.BlockSpec(memory_space=pltpu.VMEM)
    anywhere = pl.BlockSpec(memory_space=pl.ANY)
    chunks = call(z_forward_kernel, shape(2048, 128))(moments, jnp.asarray(Z_FORWARD))
    chunks = chunks.reshape(8, 256, 128)
    far, mid = call(lift_kernel, (shape(256, 128), shape(256, 128)))(
        chunks[2], chunks[4], swap(chunks[3], 1), swap(chunks[5], 1)
    )
    near = swap(chunks[6:8].reshape(512, 128), 2)
    own, across = call(meet_kernel, (shape(256, 128), shape(256, 128)), (), [whole] * 2 + [anywhere] * 3)(
        chunks[0:2].reshape(512, 128), near, far, mid, mirror
    )
    received = [own, swap(far, 4), swap(mid, 6), swap(across, 1)]

    kernels, couplings = call(prepare_kernel, (shape(2, 2, 128, 640), shape(384, 640, dtype=BF)))(
        kernel, mirror, jnp.pad(coupling, ((0, 32 - NC), (0, 32 - NC))), jnp.asarray(EXPAND)
    )

    along = call(y_forward_kernel, shape(512, 128), (), [whole] * 5 + [anywhere])(*received, jnp.asarray(Y_FORWARD), kernels)
    along = lax.all_to_all(along.reshape(32, 16, 128), "wide", split_axis=0, concat_axis=0, tiled=True)
    along = call(middle_kernel, shape(32, 2, 8, 128))(
        along.reshape(32, 2, 8, 128), jnp.asarray(X_FORWARD), couplings, kernels, jnp.asarray(X_INVERSE)
    )
    along = lax.all_to_all(along.reshape(32, 16, 128), "wide", split_axis=0, concat_axis=0, tiled=True)
    plane = call(y_inverse_kernel, shape(256, 128))(along.reshape(512, 128), jnp.asarray(Y_INVERSE))

    other = shift(plane, ACROSS)
    far = shift(plane, FAR)
    above, below = shift(plane, ABOVE), shift(plane, BELOW)
    far_other, above_other, below_other = shift(far, ACROSS), shift(other, ABOVE), shift(other, BELOW)
    planes = [plane, far, above, below, other, far_other, above_other, below_other]
    local = call(z_inverse_kernel, shape(NC * 64, 128), [pltpu.VMEM((2048, 128), F32)])(*planes, jnp.asarray(Z_INVERSE))
    children = call(
        tail_kernel,
        shape(NC, 64, 128),
        [pltpu.VMEM((256, 128), F32), pltpu.VMEM((NC * 64, 128), F32), pltpu.SemaphoreType.DMA((2,))],
        [whole] * 3,
        pl.BlockSpec(memory_space=pltpu.HBM),
    )(local, octants, l2l)
    children = children.reshape(NC, 32, 2, 128).swapaxes(1, 2)
    return children.reshape(1, NC, 2, 4096)


def solution(mesh):
    return jax.shard_map(
        shards,
        mesh=mesh,
        in_specs=(
            P("narrow", None, "wide", None),
            P("narrow", "wide", None),
            P("narrow", "wide", None),
            P(),
            P(),
            P(None, None, None, "wide", "narrow"),
            P(),
        ),
        out_specs=P("narrow", None, "wide", None),
        check_vma=False,
    )
```
